512 devices in a mesh: seq: 32 (over x, z_lo, core), head: 16 (over y, z_hi).
Axes of the slice: x: 4, y: 4, z: 16 (z_hi: 4, z_lo: 4; z = z_hi * 4 + z_lo), core: 2. Of those that a mesh axis runs over, the one named last changes fastest.
Arguments:
- tokens: bfloat16 [16384, 1152], P(('seq', 'head')), may hold values from -1.796875 to 1.796875
- qkv: bfloat16 [16384, 3456], P(('seq', 'head')), may hold values from -96 to 96, as said below
- out_weight: bfloat16 [1152, 1152], P(None, 'seq'), may hold values from -0.1875 to 0.1875
- out_bias: float32 [1152], replicated, may hold values from -1 to 1
- gate_table: bfloat16 [1000, 1152], replicated, may hold values from -5 to 5
- timesteps: int32 [4], replicated, may hold values from 0 to 999
- tile_mask: int32 [128, 128], replicated, may hold values from 0 to 1, as said below
Outputs:
- mixed: bfloat16 [16384, 1152], P(('seq', 'head'))
The draws below stay inside these ranges and needn't reach their ends.
Inputs may be any that keep to these rules, and one draw needn't show every extreme that they name: `qkv`: columns are grouped by head: for each of the 16 heads its query, key and value, 72 columns each. `tile_mask`: A tile is 1 wherever the two tiles hold the same position within their frames (in any two frames). Otherwise a tile is 1 only where the two tiles' frames differ by at most one and their positions within their frames differ by at most 4 tiles.
All inputs are finite; a program needn't handle non-finite values.
Results may differ from the reference program's by a relative error of at most 0.009.
Values may be sent and summed in bfloat16 or wider, within the bound.
A program may use at most 128 MiB of HBM per device.

```python
import jax
import jax.numpy as jnp
from jax import lax

D = 1152
HEADS = 16
HEAD_DIM = 72
TOK_DEV = 32
TILE = 128
FRAME = 4096
TSTEPS = 1000
TOKENS = 16384
TILES = 128
FRAMES = 4
N_HEAD = 16


def draw_qkv(key, part):
    key = jax.random.fold_in(key, 11)
    shape = (TOKENS, HEADS, 3, HEAD_DIM)
    factors = jnp.array([1.5, 1.5, 1.0], jnp.float32)[None, None, :, None]
    base = jax.random.normal(key, shape, jnp.float32) * factors
    return base.reshape(TOKENS, 3 * D).astype(jnp.bfloat16)


def draw_tile_mask(key, part):
    key = jax.random.fold_in(key, 5)
    tiles = jnp.arange(TILES)
    per_frame = FRAME // TILE
    spread = per_frame // 8
    frame_ids = tiles * TILE // FRAME
    spots = tiles % per_frame
    near = (jnp.abs(frame_ids[:, None] - frame_ids[None, :]) <= 1) & (jnp.abs(spots[:, None] - spots[None, :]) <= spread)
    coins = jax.random.randint(key, (TILES, TILES), 0, 4) > 0
    same_spot = spots[:, None] == spots[None, :]
    live = near & coins | same_spot
    return live.astype(jnp.int32)


def with_ends(values, stream_key, least, top_value):
    place = [jax.random.randint(jax.random.fold_in(stream_key, axis), (), 0, length) for axis, length in enumerate(values.shape)]
    main_axis = values.shape.index(max(values.shape))
    neighbour = place[:main_axis] + [(place[main_axis] + 1) % values.shape[main_axis]] + place[main_axis + 1:]
    return values.at[tuple(place)].set(least).at[tuple(neighbour)].set(top_value)


def block_levels(own_key, shape, pieces, smallest, high):
    gain, own = 1.0, jax.random.fold_in(own_key, 6)
    for dim, shards_of in pieces:
        heights = jnp.exp(jax.random.uniform(jax.random.fold_in(own, dim), (shards_of,), jnp.float32, smallest / len(pieces), high / len(pieces)))
        gain = gain * jnp.repeat(heights, shape[dim] // shards_of).reshape([-1 if axis == dim else 1 for axis in range(len(shape))])
    return gain


def noise(rng, dims, scale, reach, split=(), kind=jnp.bfloat16):
    factor_of = block_levels(rng, dims, split, -0.22, 0.18) if split else 1.0
    values = jax.random.normal(rng, dims, jnp.float32) * scale * factor_of
    return jnp.minimum(jnp.maximum(values, -reach), reach).astype(kind)


def setup_inputs(seed: int = 0) -> dict:
    key_list = jax.random.split(jax.random.key(seed), 8)
    tokens = noise(key_list[0], (TOKENS, D), 0.3, 1.796875, ((0, 512),))
    qkv = draw_qkv(jax.random.fold_in(key_list[7], 71), 0)
    out_weight = noise(key_list[2], (D, D), D ** -0.5, 0.1875, ((1, 32),))
    out_bias = noise(key_list[3], (D,), 0.2, 1.0, (), jnp.float32)
    gate_table = noise(key_list[4], (TSTEPS, D), 1.0, 5.0)
    timesteps = with_ends(jax.random.randint(key_list[5], (FRAMES,), 0, TSTEPS), jax.random.fold_in(key_list[5], 1), 0, TSTEPS - 1).astype(jnp.int32)
    tile_mask = draw_tile_mask(jax.random.fold_in(key_list[7], 71), 0)
    return {"tokens": tokens, "qkv": qkv, "out_weight": out_weight, "out_bias": out_bias, "gate_table": gate_table, "timesteps": timesteps, "tile_mask": tile_mask}


def reference(tokens, qkv, out_weight, out_bias, gate_table, timesteps, tile_mask):
    grouped = qkv.reshape(TOKENS, HEADS, 3, HEAD_DIM)
    query = grouped[:, :, 0].astype(jnp.float32)
    keys = grouped[:, :, 1].astype(jnp.float32)
    values = grouped[:, :, 2].astype(jnp.float32)
    scale = HEAD_DIM ** -0.5
    block = TOK_DEV * N_HEAD
    count = TOKENS // block
    key_tiles = (jnp.arange(TOKENS) // TILE).astype(jnp.int32)

    def one_block(index):
        start = (index * block).astype(jnp.int32)
        rows_q = lax.dynamic_slice_in_dim(query, start, block, 0)
        row_tiles = ((start + jnp.arange(block)) // TILE).astype(jnp.int32)
        allowed = jnp.take(jnp.take(tile_mask, row_tiles, axis=0), key_tiles, axis=1) > 0
        scores = jnp.einsum("qhd,khd->hqk", rows_q, keys) * scale
        scores = jnp.where(allowed[None], scores, -1e30)
        top = jnp.max(scores, axis=-1, keepdims=True)
        weights = jnp.where(allowed[None], jnp.exp(scores - top), 0.0)
        total = jnp.sum(weights, axis=-1)
        rounded = weights.astype(jnp.bfloat16).astype(jnp.float32)
        summed = jnp.einsum("hqk,khd->qhd", rounded, values)
        result = summed / jnp.transpose(total)[:, :, None]
        return result.reshape(block, D).astype(jnp.bfloat16)

    attended = lax.map(one_block, jnp.arange(count, dtype=jnp.int32)).reshape(TOKENS, D)
    projected = jnp.dot(attended, out_weight, preferred_element_type=jnp.float32) + out_bias
    frame_ids = (jnp.arange(TOKENS) // FRAME).astype(jnp.int32)
    gate = jnp.take(gate_table, jnp.take(timesteps, frame_ids), axis=0).astype(jnp.float32)
    return (tokens.astype(jnp.float32) + gate * projected).astype(jnp.bfloat16)
```

```python
import functools
import math

import jax
import jax.numpy as jnp
from jax import lax
from jax.experimental import pallas as pl
from jax.experimental.pallas import tpu as pltpu
from jax.sharding import PartitionSpec as P

F32 = jnp.float32
BF16 = jnp.bfloat16
MESH = pl.DeviceIdType.MESH

HD = 72
TILE = 128
BLOCK = 512
KV = 2 * HD
KVR = KV + 16
GROUP = 4 * 3 * HD
GPAD = 896
COLS = 36
FAR = 1e30
C_EXP = HD ** (-0.5) * math.log2(math.e)

Z0, YK0, YQ0, X0, P0, WX0, WZ0, WC0, B0, R0, NSEM = 0, 3, 6, 9, 12, 18, 21, 24, 25, 28, 31


def body(tok_ref, qkv_ref, w_ref, bias_ref, gate_hbm, ts_ref, mask_ref, out_ref,
         zsend, zrecv, zt, ykv, yq, qbuf, qs, kvbuf, acc, mrun, bsend, brecv,
         wf, wtmp, wall, wfull, wt, psend, precv, gate_v, gate_row, send_sem, recv_sem, gate_sem):
    seq = lax.axis_index("seq")
    head = lax.axis_index("head")
    x = seq // 8
    p = lax.rem(seq, 8)
    zl = p // 2
    c = lax.rem(p, 2)
    y = head // 4
    zh = lax.rem(head, 4)
    z = zh * 4 + zl

    def at_z(new_z, core):
        nz = lax.rem(new_z + 16, 16)
        return (x * 8 + lax.rem(nz, 4) * 2 + core, y * 4 + nz // 4)

    def zpeer(d):
        return (seq, y * 4 + lax.rem(zh + d, 4))

    def ypeer(d):
        return (seq, lax.rem(y + d, 4) * 4 + zh)

    def xpeer(d):
        return (lax.rem(x + d, 4) * 8 + p, head)

    def remote(src, dst, k, dev):
        return pltpu.make_async_remote_copy(
            src_ref=src, dst_ref=dst, send_sem=send_sem.at[k], recv_sem=recv_sem.at[k],
            device_id=dev, device_id_type=MESH)

    barrier = pltpu.get_barrier_semaphore()
    far_z = jnp.where(c == 0, z + 2, z + 14)
    from_z = jnp.where(c == 0, z + 14, z + 2)
    peers = [f(d) for f in (zpeer, ypeer, xpeer) for d in (1, 2, 3)]
    peers += [at_z(z + 1, c), at_z(z + 15, c), at_z(far_z, c), at_z(from_z, c)]
    for dev in peers:
        pl.semaphore_signal(barrier, inc=1, device_id=dev, device_id_type=MESH)

    @pl.when(p > 0)
    def _():
        pl.semaphore_signal(barrier, inc=1, device_id=(seq - 1, head), device_id_type=MESH)

    @pl.when(p < 7)
    def _():
        pl.semaphore_signal(barrier, inc=1, device_id=(seq + 1, head), device_id_type=MESH)

    gate_copy = pltpu.make_async_copy(gate_hbm, gate_v, gate_sem.at[0])
    gate_copy.start()

    for g in range(4):
        first = (GROUP * g) // TILE
        off = GROUP * g - first * TILE
        tiles = -(-(off + GROUP) // TILE)
        piece = qkv_ref[:, first * TILE:(first + tiles) * TILE].astype(F32)
        if off:
            piece = pltpu.roll(piece, tiles * TILE - off, 1)
        zsend[g] = piece[:, :GPAD].astype(BF16)

    count = 13 + jnp.where(p > 0, 1, 0) + jnp.where(p < 7, 1, 0)
    pl.semaphore_wait(barrier, count)

    zcopies = []
    for d in (2, 1, 3):
        zc = remote(zsend.at[lax.rem(zh + d, 4)], zrecv.at[zh], Z0 + d - 1, zpeer(d))
        zc.start()
        zcopies.append(zc)
    zrecv[zh] = zsend[zh]

    wf[...] = jnp.zeros_like(wf)
    wf[:, 0:COLS] = w_ref[...].astype(F32)
    wtmp[...] = jnp.zeros_like(wtmp)
    for g in range(4):
        row = pl.multiple_of((g * 4 + y) * HD, 8)
        wtmp[80 * g:80 * g + HD, :] = wf[pl.ds(row, HD), :]
    for j in range(3):
        wall[c, zl, x, :, TILE * j:TILE * (j + 1)] = (
            jnp.transpose(wtmp[TILE * j:TILE * (j + 1), :])[0:48].astype(BF16))
    wx = [remote(wall.at[c, zl, x], wall.at[c, zl, x], WX0 + d - 1, xpeer(d)) for d in (1, 2, 3)]
    for w in wx:
        w.start()

    for f in range(4):
        kvbuf[f, KV:KVR, :] = jnp.ones((KVR - KV, 3 * BLOCK), BF16)

    @pl.when(p == 0)
    def _():
        for f in range(4):
            kvbuf[f, 0:KV, 0:BLOCK] = jnp.zeros((KV, BLOCK), BF16)

    @pl.when(p == 7)
    def _():
        for f in range(4):
            kvbuf[f, 0:KV, 2 * BLOCK:3 * BLOCK] = jnp.zeros((KV, BLOCK), BF16)

    gate_copy.wait()
    step = ts_ref[x]
    one_hot = (lax.broadcasted_iota(jnp.int32, (16, 1000), 1) == step).astype(F32).astype(BF16)
    gate_row[...] = jnp.dot(one_hot, gate_v[...], preferred_element_type=F32)

    for zc in zcopies:
        zc.wait()

    for j in range(GPAD // TILE):
        part = zrecv[:, :, TILE * j:TILE * (j + 1)].reshape(TILE, TILE).astype(F32)
        zt[TILE * j:TILE * (j + 1), :] = jnp.transpose(part)
    for g in range(4):
        ykv[g] = zt[3 * HD * g + HD:3 * HD * (g + 1), :].astype(BF16)
        yq[g] = jnp.concatenate(
            [zt[3 * HD * g:3 * HD * g + HD, :], jnp.zeros((8, TILE), F32)], axis=0).astype(BF16)
    own_lane = pl.multiple_of(BLOCK + y * TILE, TILE)
    ycopies = []
    for d in (2, 1, 3):
        dest = lax.rem(y + d, 4)
        yc = remote(ykv.at[dest], kvbuf.at[x, 0:KV, pl.ds(own_lane, TILE)], YK0 + d - 1, ypeer(d))
        yc.start()
        ycopies.append(yc)
    for d in (2, 1, 3):
        dest = lax.rem(y + d, 4)
        yc = remote(yq.at[dest], qbuf.at[y], YQ0 + d - 1, ypeer(d))
        yc.start()
        ycopies.append(yc)
    kvbuf[x, 0:KV, pl.ds(own_lane, TILE)] = ykv[y]
    qbuf[y] = yq[y]

    for w in wx:
        w.wait()
    group = wall.at[c, zl]
    wz = [remote(group, group, WZ0, at_z(z + 1, c)),
          remote(group, group, WZ0 + 1, at_z(z + 15, c)),
          remote(group, group, WZ0 + 2, at_z(far_z, c))]
    for w in wz:
        w.start()

    for yc in ycopies[:3]:
        yc.wait()

    center = kvbuf.at[x, 0:KV, BLOCK:2 * BLOCK]
    xcopies = {d: remote(center, center, X0 + d - 1, xpeer(d)) for d in (1, 2, 3)}
    for d in (1, 3, 2):
        xcopies[d].start()

    def side_copy(side, rel, frame):
        src = kvbuf.at[frame, 0:KV, BLOCK:2 * BLOCK]
        if side == 0:
            return remote(src, kvbuf.at[frame, 0:KV, 0:BLOCK], P0 + rel, (seq + 1, head))
        return remote(src, kvbuf.at[frame, 0:KV, 2 * BLOCK:3 * BLOCK], P0 + 3 + rel, (seq - 1, head))

    frames = (x, x - 1, x + 1)
    lives = (x >= 0, x > 0, x < 3)

    def sides(rel, what):
        live = lives[rel]
        up, down = p < 7, p > 0
        for side in (0, 1):
            sends, gets = (up, down) if side == 0 else (down, up)

            @pl.when(live & (gets if what == "recv" else sends))
            def _():
                copy = side_copy(side, rel, frames[rel])
                if what == "start":
                    copy.start()
                elif what == "recv":
                    copy.wait_recv()
                else:
                    copy.wait_send()

    sides(0, "start")
    for yc in ycopies[3:]:
        yc.wait()
    for a in range(4):
        padded = jnp.concatenate([qbuf[a].astype(F32), jnp.zeros((48, TILE), F32)], axis=0)
        qs[a] = jnp.transpose(padded).astype(BF16)

    def attend(frame, tiles, first):
        @pl.loop(0, 4)
        def _(a):
            lead = 4 if tiles == 9 else 0
            base = a + 4 - lead
            lanes = pl.ds(pl.multiple_of(base * TILE, TILE), tiles * TILE)
            q = qs[a]
            s = jnp.dot(q, kvbuf[frame, 0:TILE, lanes], preferred_element_type=F32)
            top = None
            pens = []
            for t in range(tiles):
                spot = 4 * p + a - lead + t
                inside = (spot >= 0) & (spot < 32)
                live = mask_ref[4 * seq + a, frame * 32 + jnp.clip(spot, 0, 31)]
                pen = jnp.where(inside, jnp.where(live > 0, 0.0, FAR), FAR).astype(F32)
                pens.append(pen)
                val = s[:, t * TILE:(t + 1) * TILE] - pen
                top = val if top is None else jnp.maximum(top, val)
            m = jnp.max(top, axis=1, keepdims=True)
            if not first:
                old = mrun[a][:, 0:1]
                m = jnp.maximum(m, old)
            mc = m * C_EXP
            weights = jnp.concatenate(
                [jnp.exp2(s[:, t * TILE:(t + 1) * TILE] * C_EXP - (mc + pens[t])).astype(BF16)
                 for t in range(tiles)], axis=1)
            got = lax.dot_general(weights, kvbuf[frame, :, lanes], (((1,), (1,)), ((), ())),
                                  preferred_element_type=F32)
            if first:
                acc[a, :, 0:KVR] = got
            else:
                acc[a, :, 0:KVR] = acc[a, :, 0:KVR] * jnp.exp2((old - m) * C_EXP) + got
            mrun[a] = jnp.broadcast_to(m, (TILE, TILE))

    sides(0, "recv")
    attend(x, 9, True)
    xcopies[1].wait_recv()
    sides(1, "start")
    xcopies[3].wait_recv()
    sides(2, "start")
    for w in wz:
        w.wait()
    wc = remote(wall.at[c], wall.at[c], WC0, (seq + 1 - 2 * c, head))
    wc.start()
    xcopies[2].wait_recv()
    attend(lax.rem(x + 2, 4), 1, False)
    sides(1, "recv")

    @pl.when(x > 0)
    def _():
        attend(x - 1, 9, False)

    @pl.when(x == 0)
    def _():
        attend(3, 1, False)

    sides(2, "recv")

    @pl.when(x < 3)
    def _():
        attend(x + 1, 9, False)

    @pl.when(x == 3)
    def _():
        attend(0, 1, False)

    bcopies = []
    for g in range(4):
        rows = acc[:, 32 * g:32 * (g + 1), :].reshape(TILE, 2 * TILE)
        low = jnp.transpose(rows[:, 0:TILE])
        high = jnp.transpose(rows[:, TILE:2 * TILE])
        total = high[KV - TILE:KV - TILE + 1]
        feats = jnp.concatenate([low[HD:TILE], high[0:KV - TILE]], axis=0) / total
        bsend[g] = jnp.concatenate([feats, jnp.zeros((8, TILE), F32)], axis=0).astype(BF16)
    for d in (2, 1, 3):
        bc = remote(bsend.at[lax.rem(zh + d, 4)], brecv.at[zh], B0 + d - 1, zpeer(d))
        bc.start()
        bcopies.append(bc)
    brecv[zh] = bsend[zh]

    wc.wait()
    for s in range(32):
        piece = wall[s % 2, (s % 8) // 2, s // 8]
        wfull[COLS * s:COLS * (s + 1), :] = piece[0:COLS].astype(F32)
    wt[...] = wfull[...].astype(BF16)

    for bc in bcopies:
        bc.wait()
    feats = jnp.concatenate(
        [brecv[...].reshape(320, TILE).astype(F32), jnp.zeros((64, TILE), F32)], axis=0)
    att = jnp.concatenate(
        [jnp.transpose(feats[TILE * j:TILE * (j + 1)]) for j in range(3)], axis=1).astype(BF16)
    acc2 = lax.dot_general(att, wt[...], (((1,), (1,)), ((), ())), preferred_element_type=F32)
    psum = acc2
    for g in range(4):
        psend[g] = psum[32 * g:32 * (g + 1)].astype(BF16)
    rcopies = []
    for d in (2, 1, 3):
        rc = remote(psend.at[lax.rem(y + d, 4)], precv.at[d - 1], R0 + d - 1, ypeer(d))
        rc.start()
        rcopies.append(rc)
    own = jnp.where(y == 0, psum[0:32], jnp.where(y == 1, psum[32:64], jnp.where(y == 2, psum[64:96], psum[96:128])))
    own = own + bias_ref[...]
    for rc in rcopies:
        rc.wait()
    proj = own + precv[0].astype(F32) + precv[1].astype(F32) + precv[2].astype(F32)
    out_ref[...] = (tok_ref[...].astype(F32) + gate_row[0:1, :] * proj).astype(BF16)

    for d in (1, 2, 3):
        xcopies[d].wait_send()
    for rel in range(3):
        sides(rel, "send")


def shards(tokens, qkv, out_weight, out_bias, gate_table, timesteps, tile_mask):
    d = tokens.shape[1]
    vm = pl.BlockSpec(memory_space=pltpu.VMEM)
    sm = pl.BlockSpec(memory_space=pltpu.SMEM)
    return pl.pallas_call(
        body,
        out_shape=jax.ShapeDtypeStruct(tokens.shape, BF16),
        in_specs=[vm, vm, vm, vm, pl.BlockSpec(memory_space=pl.ANY), sm, sm],
        out_specs=vm,
        scratch_shapes=[
            pltpu.VMEM((4, 32, GPAD), BF16),
            pltpu.VMEM((4, 32, GPAD), BF16),
            pltpu.VMEM((GPAD, TILE), F32),
            pltpu.VMEM((4, KV, TILE), BF16),
            pltpu.VMEM((4, 80, TILE), BF16),
            pltpu.VMEM((4, 80, TILE), BF16),
            pltpu.VMEM((4, TILE, TILE), BF16),
            pltpu.VMEM((4, KVR, 3 * BLOCK), BF16),
            pltpu.VMEM((4, TILE, 2 * TILE), F32),
            pltpu.VMEM((4, TILE, TILE), F32),
            pltpu.VMEM((4, 80, TILE), BF16),
            pltpu.VMEM((4, 80, TILE), BF16),
            pltpu.VMEM((d, TILE), F32),
            pltpu.VMEM((384, TILE), F32),
            pltpu.VMEM((2, 4, 4, 48, 384), BF16),
            pltpu.VMEM((d, 384), F32),
            pltpu.VMEM((d, 384), BF16),
            pltpu.VMEM((4, 32, d), BF16),
            pltpu.VMEM((3, 32, d), BF16),
            pltpu.VMEM(gate_table.shape, BF16),
            pltpu.VMEM((16, d), F32),
            pltpu.SemaphoreType.DMA((NSEM,)),
            pltpu.SemaphoreType.DMA((NSEM,)),
            pltpu.SemaphoreType.DMA((1,)),
        ],
        compiler_params=pltpu.CompilerParams(
            collective_id=0, has_side_effects=True, vmem_limit_bytes=40 * 1024 * 1024),
    )(tokens, qkv, out_weight, out_bias.reshape(1, d), gate_table, timesteps, tile_mask)


def solution(mesh):
    return jax.shard_map(
        shards,
        mesh=mesh,
        in_specs=(
            P(("seq", "head"), None),
            P(("seq", "head"), None),
            P(None, "seq"),
            P(),
            P(),
            P(),
            P(),
        ),
        out_specs=P(("seq", "head"), None),
        check_vma=False,
    )
```

```python
import functools
import math

import jax
import jax.numpy as jnp
from jax import lax
from jax.experimental import pallas as pl
from jax.experimental.pallas import tpu as pltpu
from jax.sharding import PartitionSpec as P

F32 = jnp.float32
BF16 = jnp.bfloat16
MESH = pl.DeviceIdType.MESH

HD = 72
TILE = 128
BLOCK = 512
KV = 2 * HD
KVR = KV + 16
GROUP = 4 * 3 * HD
GPAD = 896
CUT = 640
COLS = 36
FAR = 1e30
C_EXP = HD ** (-0.5) * math.log2(math.e)

ZA, ZB, YK, YQ, X0, PO, PF, WZ, WX, WC, B0, R0, NSEM = 0, 3, 6, 9, 12, 24, 26, 42, 45, 48, 52, 55, 64
ORDER = (1, 3, 2)


def body(tok_hbm, qkv_hbm, w_hbm, bias_hbm, gate_hbm, ts_hbm, mask_hbm, out_ref,
         tok_ref, qkv_ref, w_ref, bias_ref, ts_ref, mask_ref, zsa, zsb, zra, zrb, zt, ykv, yq, qbuf, qs,
         kvbuf, acc, mrun, bsend, brecv, wf, wall, wfull, wt, part, psend, precv, gate_v, gate_row,
         send_sem, recv_sem, in_sem):
    seq = lax.axis_index("seq")
    head = lax.axis_index("head")
    x = seq // 8
    p = lax.rem(seq, 8)
    zl = p // 2
    c = lax.rem(p, 2)
    y = head // 4
    zh = lax.rem(head, 4)
    z = zh * 4 + zl

    def at_z(new_z, core):
        nz = lax.rem(new_z + 16, 16)
        return (x * 8 + lax.rem(nz, 4) * 2 + core, y * 4 + nz // 4)

    def zpeer(d):
        return (seq, y * 4 + lax.rem(zh + d, 4))

    def ypeer(d):
        return (seq, lax.rem(y + d, 4) * 4 + zh)

    def xpeer(d):
        return (lax.rem(x + d, 4) * 8 + p, head)

    def remote(src, dst, k, dev):
        return pltpu.make_async_remote_copy(
            src_ref=src, dst_ref=dst, send_sem=send_sem.at[k], recv_sem=recv_sem.at[k],
            device_id=dev, device_id_type=MESH)

    mask_row = pl.multiple_of((seq // 2) * 8, 8)
    loads = [pltpu.make_async_copy(src, dst, in_sem.at[k]) for k, (src, dst) in enumerate((
        (qkv_hbm, qkv_ref), (w_hbm, w_ref), (mask_hbm.at[pl.ds(mask_row, 8)], mask_ref), (ts_hbm, ts_ref),
        (gate_hbm, gate_v), (tok_hbm, tok_ref), (bias_hbm, bias_ref)))]
    for load in loads:
        load.start()

    barrier = pltpu.get_barrier_semaphore()
    far_z = jnp.where(c == 0, z + 2, z + 14)
    from_z = jnp.where(c == 0, z + 14, z + 2)
    peers = [f(d) for f in (zpeer, ypeer, xpeer) for d in (1, 2, 3)]
    peers += [at_z(z + 1, c), at_z(z + 15, c), at_z(far_z, c), at_z(from_z, c)]
    for dev in peers:
        pl.semaphore_signal(barrier, inc=1, device_id=dev, device_id_type=MESH)

    @pl.when(p > 0)
    def _():
        pl.semaphore_signal(barrier, inc=1, device_id=(seq - 1, head), device_id_type=MESH)

    @pl.when(p < 7)
    def _():
        pl.semaphore_signal(barrier, inc=1, device_id=(seq + 1, head), device_id_type=MESH)

    loads[0].wait()
    for g in range(4):
        first = (GROUP * g) // TILE
        off = GROUP * g - first * TILE
        tiles = -(-(off + GROUP) // TILE)
        piece = qkv_ref[:, first * TILE:(first + tiles) * TILE].astype(F32)
        starts = [off + 3 * HD * i for i in range(4)]
        cols = jnp.concatenate(
            [piece[:, a + HD:a + 3 * HD] for a in starts] + [piece[:, a:a + HD] for a in starts]
            + [jnp.zeros((piece.shape[0], GPAD - GROUP), F32)], axis=1)
        zsa[g] = cols[:, :CUT].astype(BF16)
        zsb[g] = cols[:, CUT:].astype(BF16)

    count = 13 + jnp.where(p > 0, 1, 0) + jnp.where(p < 7, 1, 0)
    pl.semaphore_wait(barrier, count)

    def start_z(src, dst, base):
        copies = []
        for d in (2, 1, 3):
            zc = remote(src.at[lax.rem(zh + d, 4)], dst.at[zh], base + d - 1, zpeer(d))
            zc.start()
            copies.append(zc)
        dst[zh] = src[zh]
        return copies

    za = start_z(zsa, zra, ZA)

    loads[1].wait()
    wf[COLS:48, :] = jnp.zeros((48 - COLS, wf.shape[1]), F32)
    wf[0:COLS, :] = w_ref[...].astype(F32)
    wide = wf[...]
    lane = lax.broadcasted_iota(jnp.int32, (48, 384), 1)
    shard = jnp.zeros((48, 384), F32)
    for g in range(4):
        turned = pltpu.roll(wide, lax.rem(wf.shape[1] + 80 * g - (g * 4 + y) * HD, wf.shape[1]), 1)[:, 0:384]
        shard = jnp.where((lane >= 80 * g) & (lane < 80 * g + HD), turned, shard)
    wall[c, x, zl] = shard.astype(BF16)
    own_shard = wall.at[c, x, zl]
    wz = [remote(own_shard, own_shard, WZ, at_z(z + 1, c)),
          remote(own_shard, own_shard, WZ + 1, at_z(z + 15, c)),
          remote(own_shard, own_shard, WZ + 2, at_z(far_z, c))]

    for f in range(4):
        kvbuf[f, KV:KVR, :] = jnp.ones((KVR - KV, 3 * BLOCK), BF16)

    @pl.when(p == 0)
    def _():
        for f in range(4):
            kvbuf[f, 0:KV, 0:BLOCK] = jnp.zeros((KV, BLOCK), BF16)

    @pl.when(p == 7)
    def _():
        for f in range(4):
            kvbuf[f, 0:KV, 2 * BLOCK:3 * BLOCK] = jnp.zeros((KV, BLOCK), BF16)

    for load in loads[2:]:
        load.wait()
    step = ts_ref[x]
    one_hot = (lax.broadcasted_iota(jnp.int32, (16, 1000), 1) == step).astype(F32).astype(BF16)
    gate_row[...] = jnp.dot(one_hot, gate_v[...], preferred_element_type=F32)

    for zc in za:
        zc.wait_send()
    zb = start_z(zsb, zrb, ZB)
    for zc in za:
        zc.wait_recv()

    for j in range(CUT // TILE):
        turn = zra[:, :, TILE * j:TILE * (j + 1)].reshape(TILE, TILE).astype(F32)
        zt[TILE * j:TILE * (j + 1), :] = jnp.transpose(turn)
    for g in range(4):
        ykv[g] = zt[KV * g:KV * (g + 1), :].astype(BF16)

    tiles_of = [y, lax.rem(y + 3, 4), lax.rem(y + 1, 4), lax.rem(y + 2, 4)]
    lanes_of = [pl.ds(pl.multiple_of(BLOCK + t * TILE, TILE), TILE) for t in tiles_of]
    ycopies = []
    for d in ORDER:
        yc = remote(ykv.at[lax.rem(y + d, 4)], kvbuf.at[x, 0:KV, lanes_of[0]], YK + d - 1, ypeer(d))
        yc.start()
        ycopies.append(yc)
    kvbuf[x, 0:KV, lanes_of[0]] = ykv[y]
    for w in wz:
        w.start()

    xcopies = {}
    for k in range(4):
        if k:
            ycopies[k - 1].wait()
        for d in ORDER:
            ref = kvbuf.at[x, 0:KV, lanes_of[k]]
            xcopies[d, k] = remote(ref, ref, X0 + 4 * (d - 1) + k, xpeer(d))
            xcopies[d, k].start()

    frames = (x, x - 1, x + 1)
    lives = (x >= 0, x > 0, x < 3)
    up, down = p < 7, p > 0

    def own_side(side):
        src = kvbuf.at[x, 0:KV, BLOCK:2 * BLOCK]
        if side == 0:
            return remote(src, kvbuf.at[x, 0:KV, 0:BLOCK], PO, (seq + 1, head))
        return remote(src, kvbuf.at[x, 0:KV, 2 * BLOCK:3 * BLOCK], PO + 1, (seq - 1, head))

    def pass_on(side, rel, k):
        src = kvbuf.at[frames[rel], 0:KV, lanes_of[k]]
        shift = -BLOCK if side == 0 else BLOCK
        lanes = pl.ds(pl.multiple_of(BLOCK + shift + tiles_of[k] * TILE, TILE), TILE)
        return remote(src, kvbuf.at[frames[rel], 0:KV, lanes], PF + (side * 2 + rel - 1) * 4 + k,
                      (seq + 1 - 2 * side, head))

    @pl.when(up)
    def _():
        own_side(0).start()

    @pl.when(down)
    def _():
        own_side(1).start()

    for zc in zb:
        zc.wait()
    for j in range((GPAD - CUT) // TILE):
        turn = zrb[:, :, TILE * j:TILE * (j + 1)].reshape(TILE, TILE).astype(F32)
        zt[CUT + TILE * j:CUT + TILE * (j + 1), :] = jnp.transpose(turn)
    for g in range(4):
        row = 4 * KV + HD * g
        yq[g] = jnp.concatenate([zt[row:row + HD, :], jnp.zeros((8, TILE), F32)], axis=0).astype(BF16)
    qcopies = []
    for d in ORDER:
        qc = remote(yq.at[lax.rem(y + d, 4)], qbuf.at[y], YQ + d - 1, ypeer(d))
        qc.start()
        qcopies.append(qc)
    qbuf[y] = yq[y]

    for w in wz:
        w.wait()
    group = wall.at[c, x]
    wx = {d: remote(group, group, WX + d - 1, xpeer(d)) for d in ORDER}
    for d in ORDER:
        wx[d].start()
    other = (seq + 1 - 2 * c, head)
    wc = [remote(group, group, WC, other)]
    wc[0].start()

    for qc in qcopies:
        qc.wait()
    for a in range(4):
        padded = jnp.concatenate([qbuf[a].astype(F32), jnp.zeros((48, TILE), F32)], axis=0)
        qs[a] = jnp.transpose(padded).astype(BF16)

    def attend(frame, tiles, first):
        @pl.loop(0, 4, unroll=True)
        def _(a):
            lead = 4 if tiles == 9 else 0
            base = a + 4 - lead
            lanes = pl.ds(pl.multiple_of(base * TILE, TILE), tiles * TILE)
            q = qs[a]
            s = jnp.dot(q, kvbuf[frame, 0:TILE, lanes], preferred_element_type=F32)
            top = None
            pens = []
            for t in range(tiles):
                spot = 4 * p + a - lead + t
                inside = (spot >= 0) & (spot < 32)
                live = mask_ref[4 * lax.rem(seq, 2) + a, frame * 32 + jnp.clip(spot, 0, 31)]
                pen = jnp.where(inside, jnp.where(live > 0, 0.0, FAR), FAR).astype(F32)
                pens.append(pen)
                val = s[:, t * TILE:(t + 1) * TILE] - pen
                top = val if top is None else jnp.maximum(top, val)
            m = jnp.max(top, axis=1, keepdims=True)
            if not first:
                old = mrun[a][:, 0:1]
                m = jnp.maximum(m, old)
            mc = m * C_EXP
            weights = jnp.concatenate(
                [jnp.exp2(s[:, t * TILE:(t + 1) * TILE] * C_EXP - (mc + pens[t])).astype(BF16)
                 for t in range(tiles)], axis=1)
            got = lax.dot_general(weights, kvbuf[frame, :, lanes], (((1,), (1,)), ((), ())),
                                  preferred_element_type=F32)
            if first:
                acc[a, :, 0:KVR] = got
            else:
                acc[a, :, 0:KVR] = acc[a, :, 0:KVR] * jnp.exp2((old - m) * C_EXP) + got
            mrun[a] = jnp.broadcast_to(m, (TILE, TILE))

    for k in range(4):
        for rel, d in ((1, 1), (2, 3)):
            xcopies[d, k].wait_recv()
            for side, gate_on in ((0, up), (1, down)):
                @pl.when(lives[rel] & gate_on)
                def _():
                    pass_on(side, rel, k).start()

    @pl.when(down)
    def _():
        own_side(0).wait_recv()

    @pl.when(up)
    def _():
        own_side(1).wait_recv()

    attend(x, 9, True)

    for k in range(4):
        xcopies[2, k].wait_recv()
    attend(lax.rem(x + 2, 4), 1, False)

    def passed(rel):
        for side, gate_on in ((0, down), (1, up)):
            @pl.when(lives[rel] & gate_on)
            def _():
                for k in range(4):
                    pass_on(side, rel, k).wait_recv()

    passed(1)

    @pl.when(x > 0)
    def _():
        attend(x - 1, 9, False)

    @pl.when(x == 0)
    def _():
        attend(3, 1, False)

    passed(2)

    @pl.when(x < 3)
    def _():
        attend(x + 1, 9, False)

    @pl.when(x == 3)
    def _():
        attend(0, 1, False)

    def finished(g):
        rows = acc[:, pl.ds(pl.multiple_of(32 * g, 32), 32), :].reshape(TILE, 2 * TILE)
        low = jnp.transpose(rows[:, 0:TILE])
        high = jnp.transpose(rows[:, TILE:2 * TILE])
        total = high[KV - TILE:KV - TILE + 1]
        feats = jnp.concatenate([low[HD:TILE], high[0:KV - TILE]], axis=0) / total
        return jnp.concatenate([feats, jnp.zeros((8, TILE), F32)], axis=0).astype(BF16)

    bcopies = []
    for d in (2, 1, 3):
        dest = lax.rem(zh + d, 4)
        bsend[d] = finished(dest)
        bc = remote(bsend.at[d], brecv.at[zh], B0 + d - 1, zpeer(d))
        bc.start()
        bcopies.append(bc)
    brecv[zh] = finished(zh)

    for n, d in enumerate(ORDER):
        wx[d].wait()
        got_x = wall.at[c, lax.rem(x + 4 - d, 4)]
        wc.append(remote(got_x, got_x, WC + 1 + n, other))
        wc[-1].start()
    for n, d in enumerate((0,) + ORDER):
        wc[n].wait()
        frm = lax.rem(x + 4 - d, 4)
        for s in range(8):
            piece = wall[s % 2, frm, s // 2]
            wfull[COLS * s:COLS * (s + 1), :] = piece[0:COLS].astype(F32)
        wt[pl.ds(pl.multiple_of(288 * frm, 32), 288), :] = wfull[...].astype(BF16)

    for bc in bcopies:
        bc.wait()

    feats = jnp.concatenate(
        [brecv[...].reshape(320, TILE).astype(F32), jnp.zeros((64, TILE), F32)], axis=0)
    att = jnp.concatenate(
        [jnp.transpose(feats[TILE * j:TILE * (j + 1)]) for j in range(3)], axis=1).astype(BF16)
    rcopies = []
    for j in range(3):
        res = lax.dot_general(att, wt[384 * j:384 * (j + 1)], (((1,), (1,)), ((), ())),
                              preferred_element_type=F32)
        part[j] = res
        for g in range(4):
            psend[j, g] = res[32 * g:32 * (g + 1)].astype(BF16)
        for d in (2, 1, 3):
            rc = remote(psend.at[j, lax.rem(y + d, 4)], precv.at[j, d - 1], R0 + 3 * j + d - 1, ypeer(d))
            rc.start()
            rcopies.append(rc)

    for j in range(3):
        for rc in rcopies[3 * j:3 * j + 3]:
            rc.wait()
        cols = slice(384 * j, 384 * (j + 1))
        proj = part[j, pl.ds(pl.multiple_of(32 * y, 32), 32), :] + bias_ref[cols].reshape(1, -1)
        for d in range(3):
            proj = proj + precv[j, d].astype(F32)
        out_ref[:, cols] = (tok_ref[:, cols].astype(F32) + gate_row[0:1, cols] * proj).astype(BF16)

    for copy in xcopies.values():
        copy.wait_send()
    for side, gate_on in ((0, up), (1, down)):
        @pl.when(gate_on)
        def _():
            own_side(side).wait_send()

        for rel in (1, 2):
            @pl.when(lives[rel] & gate_on)
            def _():
                for k in range(4):
                    pass_on(side, rel, k).wait_send()


def shards(tokens, qkv, out_weight, out_bias, gate_table, timesteps, tile_mask):
    d = tokens.shape[1]
    vm = pl.BlockSpec(memory_space=pltpu.VMEM)
    hbm = pl.BlockSpec(memory_space=pltpu.HBM)
    return pl.pallas_call(
        body,
        out_shape=jax.ShapeDtypeStruct(tokens.shape, BF16),
        in_specs=[hbm] * 7,
        out_specs=vm,
        scratch_shapes=[
            pltpu.VMEM(tokens.shape, BF16),
            pltpu.VMEM(qkv.shape, BF16),
            pltpu.VMEM(out_weight.shape[::-1], BF16),
            pltpu.VMEM((d,), F32),
            pltpu.SMEM(timesteps.shape, jnp.int32),
            pltpu.SMEM((8, tile_mask.shape[1]), jnp.int32),
            pltpu.VMEM((4, 32, CUT), BF16),
            pltpu.VMEM((4, 32, GPAD - CUT), BF16),
            pltpu.VMEM((4, 32, CUT), BF16),
            pltpu.VMEM((4, 32, GPAD - CUT), BF16),
            pltpu.VMEM((GPAD, TILE), F32),
            pltpu.VMEM((4, KV, TILE), BF16),
            pltpu.VMEM((4, 80, TILE), BF16),
            pltpu.VMEM((4, 80, TILE), BF16),
            pltpu.VMEM((4, TILE, TILE), BF16),
            pltpu.VMEM((4, KVR, 3 * BLOCK), BF16),
            pltpu.VMEM((4, TILE, 2 * TILE), F32),
            pltpu.VMEM((4, TILE, TILE), F32),
            pltpu.VMEM((4, 80, TILE), BF16),
            pltpu.VMEM((4, 80, TILE), BF16),
            pltpu.VMEM((48, d), F32),
            pltpu.VMEM((2, 4, 4, 48, 384), BF16),
            pltpu.VMEM((288, 384), F32),
            pltpu.VMEM((d, 384), BF16),
            pltpu.VMEM((3, TILE, 384), F32),
            pltpu.VMEM((3, 4, 32, 384), BF16),
            pltpu.VMEM((3, 3, 32, 384), BF16),
            pltpu.VMEM(gate_table.shape, BF16),
            pltpu.VMEM((16, d), F32),
            pltpu.SemaphoreType.DMA((NSEM,)),
            pltpu.SemaphoreType.DMA((NSEM,)),
            pltpu.SemaphoreType.DMA((7,)),
        ],
        compiler_params=pltpu.CompilerParams(
            collective_id=0, has_side_effects=True, vmem_limit_bytes=63 * 1024 * 1024),
    )(tokens, qkv, out_weight.T, out_bias, gate_table, timesteps, tile_mask)


def solution(mesh):
    return jax.shard_map(
        shards,
        mesh=mesh,
        in_specs=(
            P(("seq", "head"), None),
            P(("seq", "head"), None),
            P(None, "seq"),
            P(),
            P(),
            P(),
            P(),
        ),
        out_specs=P(("seq", "head"), None),
        check_vma=False,
    )
```

```python
import functools
import math

import jax
import jax.numpy as jnp
from jax import lax
from jax.experimental import pallas as pl
from jax.experimental.pallas import tpu as pltpu
from jax.sharding import PartitionSpec as P

F32 = jnp.float32
BF16 = jnp.bfloat16
MESH = pl.DeviceIdType.MESH

HD = 72
TILE = 128
BLOCK = 512
KV = 2 * HD
KVR = KV + 16
GROUP = 4 * 3 * HD
GPAD = 896
CUT = 640
COLS = 36
FAR = 1e30
C_EXP = HD ** (-0.5) * math.log2(math.e)

ZA, ZB, YK, YQ, X0, PO, PF, WZ, WX, WC, B0, R0, NSEM = 0, 3, 6, 9, 12, 24, 26, 42, 45, 48, 52, 55, 64
ORDER = (1, 3, 2)


def body(tok_hbm, qkv_hbm, w_hbm, bias_hbm, gate_hbm, ts_hbm, mask_hbm, out_ref,
         tok_ref, qkv_ref, w_ref, bias_ref, ts_ref, mask_ref, zsa, zsb, zra, zrb, zt, ykv, yq, qbuf, qs,
         kvbuf, acc, mrun, bsend, brecv, wf, wall, wfull, wt, part, psend, precv, gate_v, gate_row,
         send_sem, recv_sem, in_sem):
    seq = lax.axis_index("seq")
    head = lax.axis_index("head")
    x = seq // 8
    p = lax.rem(seq, 8)
    zl = p // 2
    c = lax.rem(p, 2)
    y = head // 4
    zh = lax.rem(head, 4)
    z = zh * 4 + zl

    def at_z(new_z, core):
        nz = lax.rem(new_z + 16, 16)
        return (x * 8 + lax.rem(nz, 4) * 2 + core, y * 4 + nz // 4)

    def zpeer(d):
        return (seq, y * 4 + lax.rem(zh + d, 4))

    def ypeer(d):
        return (seq, lax.rem(y + d, 4) * 4 + zh)

    def xpeer(d):
        return (lax.rem(x + d, 4) * 8 + p, head)

    def remote(src, dst, k, dev):
        return pltpu.make_async_remote_copy(
            src_ref=src, dst_ref=dst, send_sem=send_sem.at[k], recv_sem=recv_sem.at[k],
            device_id=dev, device_id_type=MESH)

    mask_row = pl.multiple_of((seq // 2) * 8, 8)
    loads = [pltpu.make_async_copy(src, dst, in_sem.at[k]) for k, (src, dst) in enumerate((
        (qkv_hbm, qkv_ref), (w_hbm, w_ref), (mask_hbm.at[pl.ds(mask_row, 8)], mask_ref), (ts_hbm, ts_ref),
        (gate_hbm, gate_v), (tok_hbm, tok_ref), (bias_hbm, bias_ref)))]
    for load in loads:
        load.start()

    barrier = pltpu.get_barrier_semaphore()
    far_z = jnp.where(c == 0, z + 2, z + 14)
    from_z = jnp.where(c == 0, z + 14, z + 2)
    peers = [f(d) for f in (zpeer, ypeer, xpeer) for d in (1, 2, 3)]
    peers += [at_z(z + 1, c), at_z(z + 15, c), at_z(far_z, c), at_z(from_z, c)]
    for dev in peers:
        pl.semaphore_signal(barrier, inc=1, device_id=dev, device_id_type=MESH)

    @pl.when(p > 0)
    def _():
        pl.semaphore_signal(barrier, inc=1, device_id=(seq - 1, head), device_id_type=MESH)

    @pl.when(p < 7)
    def _():
        pl.semaphore_signal(barrier, inc=1, device_id=(seq + 1, head), device_id_type=MESH)

    loads[0].wait()
    for g in range(4):
        first = (GROUP * g) // TILE
        off = GROUP * g - first * TILE
        tiles = -(-(off + GROUP) // TILE)
        piece = qkv_ref[:, first * TILE:(first + tiles) * TILE].astype(F32)
        starts = [off + 3 * HD * i for i in range(4)]
        cols = jnp.concatenate(
            [piece[:, a + HD:a + 3 * HD] for a in starts] + [piece[:, a:a + HD] for a in starts]
            + [jnp.zeros((piece.shape[0], GPAD - GROUP), F32)], axis=1)
        zsa[g] = cols[:, :CUT].astype(BF16)
        zsb[g] = cols[:, CUT:].astype(BF16)

    count = 13 + jnp.where(p > 0, 1, 0) + jnp.where(p < 7, 1, 0)
    pl.semaphore_wait(barrier, count)

    def start_z(src, dst, base):
        copies = []
        for d in (2, 1, 3):
            zc = remote(src.at[lax.rem(zh + d, 4)], dst.at[zh], base + d - 1, zpeer(d))
            zc.start()
            copies.append(zc)
        dst[zh] = src[zh]
        return copies

    za = start_z(zsa, zra, ZA)

    loads[1].wait()
    wf[COLS:48, :] = jnp.zeros((48 - COLS, wf.shape[1]), F32)
    wf[0:COLS, :] = w_ref[...].astype(F32)
    wide = wf[...]
    lane = lax.broadcasted_iota(jnp.int32, (48, 384), 1)
    shard = jnp.zeros((48, 384), F32)
    for g in range(4):
        turned = pltpu.roll(wide, lax.rem(wf.shape[1] + 80 * g - (g * 4 + y) * HD, wf.shape[1]), 1)[:, 0:384]
        shard = jnp.where((lane >= 80 * g) & (lane < 80 * g + HD), turned, shard)
    wall[c, x, zl] = shard.astype(BF16)
    own_shard = wall.at[c, x, zl]
    wz = [remote(own_shard, own_shard, WZ, at_z(z + 1, c)),
          remote(own_shard, own_shard, WZ + 1, at_z(z + 15, c)),
          remote(own_shard, own_shard, WZ + 2, at_z(far_z, c))]

    for f in range(4):
        kvbuf[f, KV:KVR, :] = jnp.ones((KVR - KV, 3 * BLOCK), BF16)

    @pl.when(p == 0)
    def _():
        for f in range(4):
            kvbuf[f, 0:KV, 0:BLOCK] = jnp.zeros((KV, BLOCK), BF16)

    @pl.when(p == 7)
    def _():
        for f in range(4):
            kvbuf[f, 0:KV, 2 * BLOCK:3 * BLOCK] = jnp.zeros((KV, BLOCK), BF16)

    for load in loads[2:]:
        load.wait()
    step = ts_ref[x]
    one_hot = (lax.broadcasted_iota(jnp.int32, (16, 1000), 1) == step).astype(F32).astype(BF16)
    gate_row[...] = jnp.dot(one_hot, gate_v[...], preferred_element_type=F32)

    for zc in za:
        zc.wait_send()
    zb = start_z(zsb, zrb, ZB)
    for zc in za:
        zc.wait_recv()

    for j in range(CUT // TILE):
        turn = zra[:, :, TILE * j:TILE * (j + 1)].reshape(TILE, TILE).astype(F32)
        zt[TILE * j:TILE * (j + 1), :] = jnp.transpose(turn)
    for g in range(4):
        ykv[g] = zt[KV * g:KV * (g + 1), :].astype(BF16)

    tiles_of = [y, lax.rem(y + 3, 4), lax.rem(y + 1, 4), lax.rem(y + 2, 4)]
    lanes_of = [pl.ds(pl.multiple_of(BLOCK + t * TILE, TILE), TILE) for t in tiles_of]
    ycopies = []
    for d in ORDER:
        yc = remote(ykv.at[lax.rem(y + d, 4)], kvbuf.at[x, 0:KV, lanes_of[0]], YK + d - 1, ypeer(d))
        yc.start()
        ycopies.append(yc)
    kvbuf[x, 0:KV, lanes_of[0]] = ykv[y]
    for w in wz:
        w.start()

    xcopies = {}
    for k in range(4):
        if k:
            ycopies[k - 1].wait()
        for d in ORDER:
            ref = kvbuf.at[x, 0:KV, lanes_of[k]]
            xcopies[d, k] = remote(ref, ref, X0 + 4 * (d - 1) + k, xpeer(d))
            xcopies[d, k].start()

    frames = (x, x - 1, x + 1)
    lives = (x >= 0, x > 0, x < 3)
    up, down = p < 7, p > 0

    def own_side(side):
        src = kvbuf.at[x, 0:KV, BLOCK:2 * BLOCK]
        if side == 0:
            return remote(src, kvbuf.at[x, 0:KV, 0:BLOCK], PO, (seq + 1, head))
        return remote(src, kvbuf.at[x, 0:KV, 2 * BLOCK:3 * BLOCK], PO + 1, (seq - 1, head))

    def pass_on(side, rel, k):
        src = kvbuf.at[frames[rel], 0:KV, lanes_of[k]]
        shift = -BLOCK if side == 0 else BLOCK
        lanes = pl.ds(pl.multiple_of(BLOCK + shift + tiles_of[k] * TILE, TILE), TILE)
        return remote(src, kvbuf.at[frames[rel], 0:KV, lanes], PF + (side * 2 + rel - 1) * 4 + k,
                      (seq + 1 - 2 * side, head))

    @pl.when(up)
    def _():
        own_side(0).start()

    @pl.when(down)
    def _():
        own_side(1).start()

    for zc in zb:
        zc.wait()
    for j in range((GPAD - CUT) // TILE):
        turn = zrb[:, :, TILE * j:TILE * (j + 1)].reshape(TILE, TILE).astype(F32)
        zt[CUT + TILE * j:CUT + TILE * (j + 1), :] = jnp.transpose(turn)
    for g in range(4):
        row = 4 * KV + HD * g
        yq[g] = jnp.concatenate([zt[row:row + HD, :], jnp.zeros((8, TILE), F32)], axis=0).astype(BF16)
    qcopies = []
    for d in ORDER:
        qc = remote(yq.at[lax.rem(y + d, 4)], qbuf.at[y], YQ + d - 1, ypeer(d))
        qc.start()
        qcopies.append(qc)
    qbuf[y] = yq[y]

    def attend(frame, tiles, first):
        @pl.loop(0, 4, unroll=True)
        def _(a):
            lead = 4 if tiles == 9 else 0
            base = a + 4 - lead
            lanes = pl.ds(pl.multiple_of(base * TILE, TILE), tiles * TILE)
            q = qs[a]
            s = jnp.dot(q, kvbuf[frame, 0:TILE, lanes], preferred_element_type=F32)
            top = None
            pens = []
            for t in range(tiles):
                spot = 4 * p + a - lead + t
                inside = (spot >= 0) & (spot < 32)
                live = mask_ref[4 * lax.rem(seq, 2) + a, frame * 32 + jnp.clip(spot, 0, 31)]
                pen = jnp.where(inside, jnp.where(live > 0, 0.0, FAR), FAR).astype(F32)
                pens.append(pen)
                val = s[:, t * TILE:(t + 1) * TILE] - pen
                top = val if top is None else jnp.maximum(top, val)
            m = jnp.max(top, axis=1, keepdims=True)
            if not first:
                old = mrun[a][:, 0:1]
                m = jnp.maximum(m, old)
            mc = m * C_EXP
            weights = jnp.concatenate(
                [jnp.exp2(s[:, t * TILE:(t + 1) * TILE] * C_EXP - (mc + pens[t])).astype(BF16)
                 for t in range(tiles)], axis=1)
            got = lax.dot_general(weights, kvbuf[frame, :, lanes], (((1,), (1,)), ((), ())),
                                  preferred_element_type=F32)
            if first:
                acc[a, :, 0:KVR] = got
            else:
                acc[a, :, 0:KVR] = acc[a, :, 0:KVR] * jnp.exp2((old - m) * C_EXP) + got
            mrun[a] = jnp.broadcast_to(m, (TILE, TILE))

    for k in range(4):
        for rel, d in ((1, 1), (2, 3)):
            xcopies[d, k].wait_recv()
            for side, gate_on in ((0, up), (1, down)):
                @pl.when(lives[rel] & gate_on)
                def _():
                    pass_on(side, rel, k).start()

    for qc in qcopies:
        qc.wait()
    for a in range(4):
        padded = jnp.concatenate([qbuf[a].astype(F32), jnp.zeros((48, TILE), F32)], axis=0)
        qs[a] = jnp.transpose(padded).astype(BF16)

    for w in wz:
        w.wait()
    group = wall.at[c, x]
    wx = {d: remote(group, group, WX + d - 1, xpeer(d)) for d in ORDER}
    for d in ORDER:
        wx[d].start()
    other = (seq + 1 - 2 * c, head)
    wc = [remote(group, group, WC, other)]
    wc[0].start()

    @pl.when(down)
    def _():
        own_side(0).wait_recv()

    @pl.when(up)
    def _():
        own_side(1).wait_recv()

    attend(x, 9, True)

    for k in range(4):
        xcopies[2, k].wait_recv()
    attend(lax.rem(x + 2, 4), 1, False)

    def passed(rel):
        for side, gate_on in ((0, down), (1, up)):
            @pl.when(lives[rel] & gate_on)
            def _():
                for k in range(4):
                    pass_on(side, rel, k).wait_recv()

    passed(1)

    @pl.when(x > 0)
    def _():
        attend(x - 1, 9, False)

    @pl.when(x == 0)
    def _():
        attend(3, 1, False)

    passed(2)

    @pl.when(x < 3)
    def _():
        attend(x + 1, 9, False)

    @pl.when(x == 3)
    def _():
        attend(0, 1, False)

    def finished(g):
        rows = acc[:, pl.ds(pl.multiple_of(32 * g, 32), 32), :].reshape(TILE, 2 * TILE)
        low = jnp.transpose(rows[:, 0:TILE])
        high = jnp.transpose(rows[:, TILE:2 * TILE])
        total = high[KV - TILE:KV - TILE + 1]
        feats = jnp.concatenate([low[HD:TILE], high[0:KV - TILE]], axis=0) / total
        return jnp.concatenate([feats, jnp.zeros((8, TILE), F32)], axis=0).astype(BF16)

    bcopies = []
    for d in (2, 1, 3):
        dest = lax.rem(zh + d, 4)
        bsend[d] = finished(dest)
        bc = remote(bsend.at[d], brecv.at[zh], B0 + d - 1, zpeer(d))
        bc.start()
        bcopies.append(bc)
    brecv[zh] = finished(zh)

    for n, d in enumerate(ORDER):
        wx[d].wait()
        got_x = wall.at[c, lax.rem(x + 4 - d, 4)]
        wc.append(remote(got_x, got_x, WC + 1 + n, other))
        wc[-1].start()
    for n, d in enumerate((0,) + ORDER):
        wc[n].wait()
        frm = lax.rem(x + 4 - d, 4)
        for s in range(8):
            piece = wall[s % 2, frm, s // 2]
            wfull[COLS * s:COLS * (s + 1), :] = piece[0:COLS].astype(F32)
        wt[pl.ds(pl.multiple_of(288 * frm, 32), 288), :] = wfull[...].astype(BF16)

    for bc in bcopies:
        bc.wait()

    feats = jnp.concatenate(
        [brecv[...].reshape(320, TILE).astype(F32), jnp.zeros((64, TILE), F32)], axis=0)
    att = jnp.concatenate(
        [jnp.transpose(feats[TILE * j:TILE * (j + 1)]) for j in range(3)], axis=1).astype(BF16)
    rcopies = []
    for j in range(3):
        res = lax.dot_general(att, wt[384 * j:384 * (j + 1)], (((1,), (1,)), ((), ())),
                              preferred_element_type=F32)
        part[j] = res
        for g in range(4):
            psend[j, g] = res[32 * g:32 * (g + 1)].astype(BF16)
        for d in (2, 1, 3):
            rc = remote(psend.at[j, lax.rem(y + d, 4)], precv.at[j, d - 1], R0 + 3 * j + d - 1, ypeer(d))
            rc.start()
            rcopies.append(rc)

    for j in range(3):
        for rc in rcopies[3 * j:3 * j + 3]:
            rc.wait()
        cols = slice(384 * j, 384 * (j + 1))
        proj = part[j, pl.ds(pl.multiple_of(32 * y, 32), 32), :] + bias_ref[cols].reshape(1, -1)
        for d in range(3):
            proj = proj + precv[j, d].astype(F32)
        out_ref[:, cols] = (tok_ref[:, cols].astype(F32) + gate_row[0:1, cols] * proj).astype(BF16)

    for copy in xcopies.values():
        copy.wait_send()
    for side, gate_on in ((0, up), (1, down)):
        @pl.when(gate_on)
        def _():
            own_side(side).wait_send()

        for rel in (1, 2):
            @pl.when(lives[rel] & gate_on)
            def _():
                for k in range(4):
                    pass_on(side, rel, k).wait_send()


def shards(tokens, qkv, out_weight, out_bias, gate_table, timesteps, tile_mask):
    d = tokens.shape[1]
    vm = pl.BlockSpec(memory_space=pltpu.VMEM)
    hbm = pl.BlockSpec(memory_space=pltpu.HBM)
    return pl.pallas_call(
        body,
        out_shape=jax.ShapeDtypeStruct(tokens.shape, BF16),
        in_specs=[hbm] * 7,
        out_specs=vm,
        scratch_shapes=[
            pltpu.VMEM(tokens.shape, BF16),
            pltpu.VMEM(qkv.shape, BF16),
            pltpu.VMEM(out_weight.shape[::-1], BF16),
            pltpu.VMEM((d,), F32),
            pltpu.SMEM(timesteps.shape, jnp.int32),
            pltpu.SMEM((8, tile_mask.shape[1]), jnp.int32),
            pltpu.VMEM((4, 32, CUT), BF16),
            pltpu.VMEM((4, 32, GPAD - CUT), BF16),
            pltpu.VMEM((4, 32, CUT), BF16),
            pltpu.VMEM((4, 32, GPAD - CUT), BF16),
            pltpu.VMEM((GPAD, TILE), F32),
            pltpu.VMEM((4, KV, TILE), BF16),
            pltpu.VMEM((4, 80, TILE), BF16),
            pltpu.VMEM((4, 80, TILE), BF16),
            pltpu.VMEM((4, TILE, TILE), BF16),
            pltpu.VMEM((4, KVR, 3 * BLOCK), BF16),
            pltpu.VMEM((4, TILE, 2 * TILE), F32),
            pltpu.VMEM((4, TILE, TILE), F32),
            pltpu.VMEM((4, 80, TILE), BF16),
            pltpu.VMEM((4, 80, TILE), BF16),
            pltpu.VMEM((48, d), F32),
            pltpu.VMEM((2, 4, 4, 48, 384), BF16),
            pltpu.VMEM((288, 384), F32),
            pltpu.VMEM((d, 384), BF16),
            pltpu.VMEM((3, TILE, 384), F32),
            pltpu.VMEM((3, 4, 32, 384), BF16),
            pltpu.VMEM((3, 3, 32, 384), BF16),
            pltpu.VMEM(gate_table.shape, BF16),
            pltpu.VMEM((16, d), F32),
            pltpu.SemaphoreType.DMA((NSEM,)),
            pltpu.SemaphoreType.DMA((NSEM,)),
            pltpu.SemaphoreType.DMA((7,)),
        ],
        compiler_params=pltpu.CompilerParams(
            collective_id=0, has_side_effects=True, vmem_limit_bytes=40 * 1024 * 1024),
    )(*[pltpu.with_memory_space_constraint(a, pltpu.HBM) for a in (
        tokens, qkv, out_weight.T, out_bias, gate_table, timesteps, tile_mask)])


def solution(mesh):
    return jax.shard_map(
        shards,
        mesh=mesh,
        in_specs=(
            P(("seq", "head"), None),
            P(("seq", "head"), None),
            P(None, "seq"),
            P(),
            P(),
            P(),
            P(),
        ),
        out_specs=P(("seq", "head"), None),
        check_vma=False,
    )
```

```python
import functools
import math

import jax
import jax.numpy as jnp
from jax import lax
from jax.experimental import pallas as pl
from jax.experimental.pallas import tpu as pltpu
from jax.sharding import PartitionSpec as P

F32 = jnp.float32
BF16 = jnp.bfloat16
MESH = pl.DeviceIdType.MESH

HD = 72
TILE = 128
BLOCK = 512
KV = 2 * HD
KVR = KV + 16
GROUP = 4 * 3 * HD
GPAD = 896
CUT = 640
COLS = 36
FAR = 1e30
C_EXP = HD ** (-0.5) * math.log2(math.e)

ZA, ZB, YK, YQ, X0, PF, WZ, WX, WC, B0, R0, NSEM = 0, 3, 6, 9, 12, 24, 48, 51, 54, 58, 61, 70
ORDER = (1, 3, 2)


def body(tok_hbm, qkv_hbm, w_hbm, bias_hbm, gate_hbm, ts_hbm, mask_hbm, out_ref,
         tok_ref, qkv_ref, w_ref, bias_ref, ts_ref, mask_ref, zsa, zsb, zra, zrb, zt, ykv, yq, qbuf, qs,
         kvbuf, acc, mrun, bsend, brecv, wf, wall, wfull, wt, part, psend, precv, gate_v, gate_row,
         send_sem, recv_sem, in_sem):
    seq = lax.axis_index("seq")
    head = lax.axis_index("head")
    x = seq // 8
    p = lax.rem(seq, 8)
    zl = p // 2
    c = lax.rem(p, 2)
    y = head // 4
    zh = lax.rem(head, 4)
    z = zh * 4 + zl

    def at_z(new_z, core):
        nz = lax.rem(new_z + 16, 16)
        return (x * 8 + lax.rem(nz, 4) * 2 + core, y * 4 + nz // 4)

    def zpeer(d):
        return (seq, y * 4 + lax.rem(zh + d, 4))

    def ypeer(d):
        return (seq, lax.rem(y + d, 4) * 4 + zh)

    def xpeer(d):
        return (lax.rem(x + d, 4) * 8 + p, head)

    def remote(src, dst, k, dev):
        return pltpu.make_async_remote_copy(
            src_ref=src, dst_ref=dst, send_sem=send_sem.at[k], recv_sem=recv_sem.at[k],
            device_id=dev, device_id_type=MESH)

    mask_row = pl.multiple_of((seq // 2) * 8, 8)
    loads = [pltpu.make_async_copy(src, dst, in_sem.at[k]) for k, (src, dst) in enumerate((
        (qkv_hbm, qkv_ref), (w_hbm, w_ref), (mask_hbm.at[pl.ds(mask_row, 8)], mask_ref), (ts_hbm, ts_ref),
        (gate_hbm, gate_v), (tok_hbm, tok_ref), (bias_hbm, bias_ref)))]
    for load in loads:
        load.start()

    barrier = pltpu.get_barrier_semaphore()
    far_z = jnp.where(c == 0, z + 2, z + 14)
    from_z = jnp.where(c == 0, z + 14, z + 2)
    peers = [f(d) for f in (zpeer, ypeer, xpeer) for d in (1, 2, 3)]
    peers += [at_z(z + 1, c), at_z(z + 15, c), at_z(far_z, c), at_z(from_z, c)]
    for dev in peers:
        pl.semaphore_signal(barrier, inc=1, device_id=dev, device_id_type=MESH)

    @pl.when(p > 0)
    def _():
        pl.semaphore_signal(barrier, inc=1, device_id=(seq - 1, head), device_id_type=MESH)

    @pl.when(p < 7)
    def _():
        pl.semaphore_signal(barrier, inc=1, device_id=(seq + 1, head), device_id_type=MESH)

    loads[0].wait()
    for g in range(4):
        first = (GROUP * g) // TILE
        off = GROUP * g - first * TILE
        tiles = -(-(off + GROUP) // TILE)
        piece = qkv_ref[:, first * TILE:(first + tiles) * TILE].astype(F32)
        starts = [off + 3 * HD * i for i in range(4)]
        cols = jnp.concatenate(
            [piece[:, a + HD:a + 3 * HD] for a in starts] + [piece[:, a:a + HD] for a in starts]
            + [jnp.zeros((piece.shape[0], GPAD - GROUP), F32)], axis=1)
        zsa[g] = cols[:, :CUT].astype(BF16)
        zsb[g] = cols[:, CUT:].astype(BF16)

    count = 13 + jnp.where(p > 0, 1, 0) + jnp.where(p < 7, 1, 0)
    pl.semaphore_wait(barrier, count)

    def start_z(src, dst, base):
        copies = []
        for d in (2, 1, 3):
            zc = remote(src.at[lax.rem(zh + d, 4)], dst.at[zh], base + d - 1, zpeer(d))
            zc.start()
            copies.append(zc)
        dst[zh] = src[zh]
        return copies

    za = start_z(zsa, zra, ZA)

    loads[1].wait()
    wf[COLS:48, :] = jnp.zeros((48 - COLS, wf.shape[1]), F32)
    wf[0:COLS, :] = w_ref[...].astype(F32)
    wide = wf[...]
    lane = lax.broadcasted_iota(jnp.int32, (48, 384), 1)
    shard = jnp.zeros((48, 384), F32)
    for g in range(4):
        turned = pltpu.roll(wide, lax.rem(wf.shape[1] + 80 * g - (g * 4 + y) * HD, wf.shape[1]), 1)[:, 0:384]
        shard = jnp.where((lane >= 80 * g) & (lane < 80 * g + HD), turned, shard)
    wall[c, x, zl] = shard.astype(BF16)
    own_shard = wall.at[c, x, zl]
    wz = [remote(own_shard, own_shard, WZ, at_z(z + 1, c)),
          remote(own_shard, own_shard, WZ + 1, at_z(z + 15, c)),
          remote(own_shard, own_shard, WZ + 2, at_z(far_z, c))]

    for w in wz:
        w.start()
    for f in range(4):
        kvbuf[f, KV:KVR, :] = jnp.ones((KVR - KV, 3 * BLOCK), BF16)

    @pl.when(p == 0)
    def _():
        for f in range(4):
            kvbuf[f, 0:KV, 0:BLOCK] = jnp.zeros((KV, BLOCK), BF16)

    @pl.when(p == 7)
    def _():
        for f in range(4):
            kvbuf[f, 0:KV, 2 * BLOCK:3 * BLOCK] = jnp.zeros((KV, BLOCK), BF16)

    for load in loads[2:]:
        load.wait()
    step = ts_ref[x]
    one_hot = (lax.broadcasted_iota(jnp.int32, (16, 1000), 1) == step).astype(F32).astype(BF16)
    gate_row[...] = jnp.dot(one_hot, gate_v[...], preferred_element_type=F32)

    for zc in za:
        zc.wait_send()
    zb = start_z(zsb, zrb, ZB)
    for zc in za:
        zc.wait_recv()

    for j in range(CUT // TILE):
        turn = zra[:, :, TILE * j:TILE * (j + 1)].reshape(TILE, TILE).astype(F32)
        zt[TILE * j:TILE * (j + 1), :] = jnp.transpose(turn)
    for g in range(4):
        ykv[g] = zt[KV * g:KV * (g + 1), :].astype(BF16)

    tiles_of = [y, lax.rem(y + 3, 4), lax.rem(y + 1, 4), lax.rem(y + 2, 4)]
    lanes_of = [pl.ds(pl.multiple_of(BLOCK + t * TILE, TILE), TILE) for t in tiles_of]
    ycopies = []
    for d in ORDER:
        yc = remote(ykv.at[lax.rem(y + d, 4)], kvbuf.at[x, 0:KV, lanes_of[0]], YK + d - 1, ypeer(d))
        yc.start()
        ycopies.append(yc)
    kvbuf[x, 0:KV, lanes_of[0]] = ykv[y]

    frames = (x, x - 1, x + 1)
    lives = (x >= 0, x > 0, x < 3)
    up, down = p < 7, p > 0

    def pass_on(side, rel, k):
        src = kvbuf.at[frames[rel], 0:KV, lanes_of[k]]
        shift = -BLOCK if side == 0 else BLOCK
        lanes = pl.ds(pl.multiple_of(BLOCK + shift + tiles_of[k] * TILE, TILE), TILE)
        return remote(src, kvbuf.at[frames[rel], 0:KV, lanes], PF + (side * 3 + rel) * 4 + k,
                      (seq + 1 - 2 * side, head))

    def pass_tile(rel, k):
        for side, gate_on in ((0, up), (1, down)):
            @pl.when(lives[rel] & gate_on)
            def _():
                pass_on(side, rel, k).start()

    xcopies = {}
    for k in range(4):
        if k:
            ycopies[k - 1].wait()
        for d in ORDER:
            ref = kvbuf.at[x, 0:KV, lanes_of[k]]
            xcopies[d, k] = remote(ref, ref, X0 + 4 * (d - 1) + k, xpeer(d))
            xcopies[d, k].start()
        pass_tile(0, k)

    for zc in zb:
        zc.wait()
    for j in range((GPAD - CUT) // TILE):
        turn = zrb[:, :, TILE * j:TILE * (j + 1)].reshape(TILE, TILE).astype(F32)
        zt[CUT + TILE * j:CUT + TILE * (j + 1), :] = jnp.transpose(turn)
    for g in range(4):
        row = 4 * KV + HD * g
        yq[g] = jnp.concatenate([zt[row:row + HD, :], jnp.zeros((8, TILE), F32)], axis=0).astype(BF16)
    qcopies = []
    for d in ORDER:
        qc = remote(yq.at[lax.rem(y + d, 4)], qbuf.at[y], YQ + d - 1, ypeer(d))
        qc.start()
        qcopies.append(qc)
    qbuf[y] = yq[y]

    def attend(frame, tiles, first):
        @pl.loop(0, 4, unroll=True)
        def _(a):
            lead = 4 if tiles == 9 else 0
            base = a + 4 - lead
            lanes = pl.ds(pl.multiple_of(base * TILE, TILE), tiles * TILE)
            q = qs[a]
            s = jnp.dot(q, kvbuf[frame, 0:TILE, lanes], preferred_element_type=F32)
            top = None
            pens = []
            for t in range(tiles):
                spot = 4 * p + a - lead + t
                inside = (spot >= 0) & (spot < 32)
                live = mask_ref[4 * lax.rem(seq, 2) + a, frame * 32 + jnp.clip(spot, 0, 31)]
                pen = jnp.where(inside, jnp.where(live > 0, 0.0, FAR), FAR).astype(F32)
                pens.append(pen)
                val = s[:, t * TILE:(t + 1) * TILE] - pen
                top = val if top is None else jnp.maximum(top, val)
            m = jnp.max(top, axis=1, keepdims=True)
            if not first:
                old = mrun[a][:, 0:1]
                m = jnp.maximum(m, old)
            mc = m * C_EXP
            weights = jnp.concatenate(
                [jnp.exp2(s[:, t * TILE:(t + 1) * TILE] * C_EXP - (mc + pens[t])).astype(BF16)
                 for t in range(tiles)], axis=1)
            got = lax.dot_general(weights, kvbuf[frame, :, lanes], (((1,), (1,)), ((), ())),
                                  preferred_element_type=F32)
            if first:
                acc[a, :, 0:KVR] = got
            else:
                acc[a, :, 0:KVR] = acc[a, :, 0:KVR] * jnp.exp2((old - m) * C_EXP) + got
            mrun[a] = jnp.broadcast_to(m, (TILE, TILE))

    for k in range(4):
        for rel, d in ((1, 1), (2, 3)):
            xcopies[d, k].wait_recv()
            pass_tile(rel, k)

    for qc in qcopies:
        qc.wait()
    for a in range(4):
        padded = jnp.concatenate([qbuf[a].astype(F32), jnp.zeros((48, TILE), F32)], axis=0)
        qs[a] = jnp.transpose(padded).astype(BF16)

    for w in wz:
        w.wait()
    group = wall.at[c, x]
    wx = {d: remote(group, group, WX + d - 1, xpeer(d)) for d in ORDER}
    for d in ORDER:
        wx[d].start()
    other = (seq + 1 - 2 * c, head)
    wc = [remote(group, group, WC, other)]
    wc[0].start()

    def passed(rel):
        for side, gate_on in ((0, down), (1, up)):
            @pl.when(lives[rel] & gate_on)
            def _():
                for k in range(4):
                    pass_on(side, rel, k).wait_recv()

    passed(0)

    attend(x, 9, True)

    for k in range(4):
        xcopies[2, k].wait_recv()
    attend(lax.rem(x + 2, 4), 1, False)

    passed(1)

    @pl.when(x > 0)
    def _():
        attend(x - 1, 9, False)

    @pl.when(x == 0)
    def _():
        attend(3, 1, False)

    passed(2)

    @pl.when(x < 3)
    def _():
        attend(x + 1, 9, False)

    @pl.when(x == 3)
    def _():
        attend(0, 1, False)

    def finished(g):
        rows = acc[:, pl.ds(pl.multiple_of(32 * g, 32), 32), :].reshape(TILE, 2 * TILE)
        low = jnp.transpose(rows[:, 0:TILE])
        high = jnp.transpose(rows[:, TILE:2 * TILE])
        total = high[KV - TILE:KV - TILE + 1]
        feats = jnp.concatenate([low[HD:TILE], high[0:KV - TILE]], axis=0) / total
        return jnp.concatenate([feats, jnp.zeros((8, TILE), F32)], axis=0).astype(BF16)

    bcopies = []
    for d in (2, 1, 3):
        dest = lax.rem(zh + d, 4)
        bsend[d] = finished(dest)
        bc = remote(bsend.at[d], brecv.at[zh], B0 + d - 1, zpeer(d))
        bc.start()
        bcopies.append(bc)
    brecv[zh] = finished(zh)

    for n, d in enumerate(ORDER):
        wx[d].wait()
        got_x = wall.at[c, lax.rem(x + 4 - d, 4)]
        wc.append(remote(got_x, got_x, WC + 1 + n, other))
        wc[-1].start()
    for n, d in enumerate((0,) + ORDER):
        wc[n].wait()
        frm = lax.rem(x + 4 - d, 4)
        for s in range(8):
            piece = wall[s % 2, frm, s // 2]
            wfull[COLS * s:COLS * (s + 1), :] = piece[0:COLS].astype(F32)
        wt[pl.ds(pl.multiple_of(288 * frm, 32), 288), :] = wfull[...].astype(BF16)

    for bc in bcopies:
        bc.wait()

    feats = jnp.concatenate(
        [brecv[...].reshape(320, TILE).astype(F32), jnp.zeros((64, TILE), F32)], axis=0)
    att = jnp.concatenate(
        [jnp.transpose(feats[TILE * j:TILE * (j + 1)]) for j in range(3)], axis=1).astype(BF16)
    rcopies = []
    for j in range(3):
        res = lax.dot_general(att, wt[384 * j:384 * (j + 1)], (((1,), (1,)), ((), ())),
                              preferred_element_type=F32)
        part[j] = res
        for g in range(4):
            psend[j, g] = res[32 * g:32 * (g + 1)].astype(BF16)
        for d in (2, 1, 3):
            rc = remote(psend.at[j, lax.rem(y + d, 4)], precv.at[j, d - 1], R0 + 3 * j + d - 1, ypeer(d))
            rc.start()
            rcopies.append(rc)

    for j in range(3):
        for rc in rcopies[3 * j:3 * j + 3]:
            rc.wait()
        cols = slice(384 * j, 384 * (j + 1))
        proj = part[j, pl.ds(pl.multiple_of(32 * y, 32), 32), :] + bias_ref[cols].reshape(1, -1)
        for d in range(3):
            proj = proj + precv[j, d].astype(F32)
        out_ref[:, cols] = (tok_ref[:, cols].astype(F32) + gate_row[0:1, cols] * proj).astype(BF16)

    for copy in xcopies.values():
        copy.wait_send()
    for rel in range(3):
        for side, gate_on in ((0, up), (1, down)):
            @pl.when(lives[rel] & gate_on)
            def _():
                for k in range(4):
                    pass_on(side, rel, k).wait_send()


def shards(tokens, qkv, out_weight, out_bias, gate_table, timesteps, tile_mask):
    d = tokens.shape[1]
    vm = pl.BlockSpec(memory_space=pltpu.VMEM)
    hbm = pl.BlockSpec(memory_space=pltpu.HBM)
    return pl.pallas_call(
        body,
        out_shape=jax.ShapeDtypeStruct(tokens.shape, BF16),
        in_specs=[hbm] * 7,
        out_specs=vm,
        scratch_shapes=[
            pltpu.VMEM(tokens.shape, BF16),
            pltpu.VMEM(qkv.shape, BF16),
            pltpu.VMEM(out_weight.shape[::-1], BF16),
            pltpu.VMEM((d,), F32),
            pltpu.SMEM(timesteps.shape, jnp.int32),
            pltpu.SMEM((8, tile_mask.shape[1]), jnp.int32),
            pltpu.VMEM((4, 32, CUT), BF16),
            pltpu.VMEM((4, 32, GPAD - CUT), BF16),
            pltpu.VMEM((4, 32, CUT), BF16),
            pltpu.VMEM((4, 32, GPAD - CUT), BF16),
            pltpu.VMEM((GPAD, TILE), F32),
            pltpu.VMEM((4, KV, TILE), BF16),
            pltpu.VMEM((4, 80, TILE), BF16),
            pltpu.VMEM((4, 80, TILE), BF16),
            pltpu.VMEM((4, TILE, TILE), BF16),
            pltpu.VMEM((4, KVR, 3 * BLOCK), BF16),
            pltpu.VMEM((4, TILE, 2 * TILE), F32),
            pltpu.VMEM((4, TILE, TILE), F32),
            pltpu.VMEM((4, 80, TILE), BF16),
            pltpu.VMEM((4, 80, TILE), BF16),
            pltpu.VMEM((48, d), F32),
            pltpu.VMEM((2, 4, 4, 48, 384), BF16),
            pltpu.VMEM((288, 384), F32),
            pltpu.VMEM((d, 384), BF16),
            pltpu.VMEM((3, TILE, 384), F32),
            pltpu.VMEM((3, 4, 32, 384), BF16),
            pltpu.VMEM((3, 3, 32, 384), BF16),
            pltpu.VMEM(gate_table.shape, BF16),
            pltpu.VMEM((16, d), F32),
            pltpu.SemaphoreType.DMA((NSEM,)),
            pltpu.SemaphoreType.DMA((NSEM,)),
            pltpu.SemaphoreType.DMA((7,)),
        ],
        compiler_params=pltpu.CompilerParams(
            collective_id=0, has_side_effects=True, vmem_limit_bytes=40 * 1024 * 1024),
    )(*[pltpu.with_memory_space_constraint(a, pltpu.HBM) for a in (
        tokens, qkv, out_weight.T, out_bias, gate_table, timesteps, tile_mask)])


def solution(mesh):
    return jax.shard_map(
        shards,
        mesh=mesh,
        in_specs=(
            P(("seq", "head"), None),
            P(("seq", "head"), None),
            P(None, "seq"),
            P(),
            P(),
            P(),
            P(),
        ),
        out_specs=P(("seq", "head"), None),
        check_vma=False,
    )
```

```python
import functools
import math

import jax
import jax.numpy as jnp
from jax import lax
from jax.experimental import pallas as pl
from jax.experimental.pallas import tpu as pltpu
from jax.sharding import PartitionSpec as P

F32 = jnp.float32
BF16 = jnp.bfloat16
MESH = pl.DeviceIdType.MESH

HD = 72
TILE = 128
BLOCK = 512
KV = 2 * HD
KVR = KV + 16
GROUP = 4 * 3 * HD
GPAD = 896
CUT = 640
COLS = 36
FAR = 1e30
C_EXP = HD ** (-0.5) * math.log2(math.e)

ZA, ZB, YK, YQ, X0, PF, WZ, WX, WC, B0, R0, NSEM = 0, 3, 6, 9, 12, 24, 48, 51, 54, 58, 61, 70
ORDER = (1, 3, 2)


def body(tok_hbm, qkv_hbm, w_hbm, bias_hbm, gate_hbm, ts_hbm, mask_hbm, out_ref,
         tok_ref, qkv_ref, w_ref, bias_ref, ts_ref, mask_ref, zsa, zsb, zra, zrb, zt, ykv, yq, qbuf, qs,
         kvbuf, acc, mrun, bsend, brecv, wf, wall, wfull, wt, part, psend, precv, gate_v, gate_row,
         send_sem, recv_sem, in_sem):
    seq = lax.axis_index("seq")
    head = lax.axis_index("head")
    x = seq // 8
    p = lax.rem(seq, 8)
    zl = p // 2
    c = lax.rem(p, 2)
    y = head // 4
    zh = lax.rem(head, 4)
    z = zh * 4 + zl

    def at_z(new_z, core):
        nz = lax.rem(new_z + 16, 16)
        return (x * 8 + lax.rem(nz, 4) * 2 + core, y * 4 + nz // 4)

    def zpeer(d):
        return (seq, y * 4 + lax.rem(zh + d, 4))

    def ypeer(d):
        return (seq, lax.rem(y + d, 4) * 4 + zh)

    def xpeer(d):
        return (lax.rem(x + d, 4) * 8 + p, head)

    def remote(src, dst, k, dev):
        return pltpu.make_async_remote_copy(
            src_ref=src, dst_ref=dst, send_sem=send_sem.at[k], recv_sem=recv_sem.at[k],
            device_id=dev, device_id_type=MESH)

    mask_row = pl.multiple_of((seq // 2) * 8, 8)
    loads = [pltpu.make_async_copy(src, dst, in_sem.at[k]) for k, (src, dst) in enumerate((
        (qkv_hbm, qkv_ref), (w_hbm, w_ref), (mask_hbm.at[pl.ds(mask_row, 8)], mask_ref), (ts_hbm, ts_ref),
        (gate_hbm, gate_v), (tok_hbm, tok_ref), (bias_hbm, bias_ref)))]
    for load in loads:
        load.start()

    barrier = pltpu.get_barrier_semaphore()
    far_z = jnp.where(c == 0, z + 2, z + 14)
    from_z = jnp.where(c == 0, z + 14, z + 2)
    peers = [f(d) for f in (zpeer, ypeer, xpeer) for d in (1, 2, 3)]
    peers += [at_z(z + 1, c), at_z(z + 15, c), at_z(far_z, c), at_z(from_z, c)]
    for dev in peers:
        pl.semaphore_signal(barrier, inc=1, device_id=dev, device_id_type=MESH)

    @pl.when(p > 0)
    def _():
        pl.semaphore_signal(barrier, inc=1, device_id=(seq - 1, head), device_id_type=MESH)

    @pl.when(p < 7)
    def _():
        pl.semaphore_signal(barrier, inc=1, device_id=(seq + 1, head), device_id_type=MESH)

    loads[0].wait()
    for g in range(4):
        first = (GROUP * g) // TILE
        off = GROUP * g - first * TILE
        tiles = -(-(off + GROUP) // TILE)
        piece = qkv_ref[:, first * TILE:(first + tiles) * TILE].astype(F32)
        starts = [off + 3 * HD * i for i in range(4)]
        cols = jnp.concatenate(
            [piece[:, a + HD:a + 3 * HD] for a in starts] + [piece[:, a:a + HD] for a in starts]
            + [jnp.zeros((piece.shape[0], GPAD - GROUP), F32)], axis=1)
        zsa[g] = cols[:, :CUT].astype(BF16)
        zsb[g] = cols[:, CUT:].astype(BF16)

    count = 13 + jnp.where(p > 0, 1, 0) + jnp.where(p < 7, 1, 0)
    pl.semaphore_wait(barrier, count)

    def start_z(src, dst, base):
        copies = []
        for d in (2, 1, 3):
            zc = remote(src.at[lax.rem(zh + d, 4)], dst.at[zh], base + d - 1, zpeer(d))
            zc.start()
            copies.append(zc)
        dst[zh] = src[zh]
        return copies

    za = start_z(zsa, zra, ZA)

    loads[1].wait()
    wf[COLS:48, :] = jnp.zeros((48 - COLS, wf.shape[1]), F32)
    wf[0:COLS, :] = w_ref[...].astype(F32)
    wide = wf[...]
    lane = lax.broadcasted_iota(jnp.int32, (48, 384), 1)
    shard = jnp.zeros((48, 384), F32)
    for g in range(4):
        turned = pltpu.roll(wide, lax.rem(wf.shape[1] + 80 * g - (g * 4 + y) * HD, wf.shape[1]), 1)[:, 0:384]
        shard = jnp.where((lane >= 80 * g) & (lane < 80 * g + HD), turned, shard)
    wall[c, x, zl] = shard.astype(BF16)
    own_shard = wall.at[c, x, zl]
    wz = [remote(own_shard, own_shard, WZ, at_z(z + 1, c)),
          remote(own_shard, own_shard, WZ + 1, at_z(z + 15, c)),
          remote(own_shard, own_shard, WZ + 2, at_z(far_z, c))]

    for w in wz:
        w.start()
    for f in range(4):
        kvbuf[f, KV:KVR, :] = jnp.ones((KVR - KV, 3 * BLOCK), BF16)

    @pl.when(p == 0)
    def _():
        for f in range(4):
            kvbuf[f, 0:KV, 0:BLOCK] = jnp.zeros((KV, BLOCK), BF16)

    @pl.when(p == 7)
    def _():
        for f in range(4):
            kvbuf[f, 0:KV, 2 * BLOCK:3 * BLOCK] = jnp.zeros((KV, BLOCK), BF16)

    for load in loads[2:]:
        load.wait()
    step = ts_ref[x]
    one_hot = (lax.broadcasted_iota(jnp.int32, (16, 1000), 1) == step).astype(F32).astype(BF16)
    gate_row[...] = jnp.dot(one_hot, gate_v[...], preferred_element_type=F32)

    for zc in za:
        zc.wait_send()
    zb = start_z(zsb, zrb, ZB)
    for zc in za:
        zc.wait_recv()

    for j in range(CUT // TILE):
        turn = zra[:, :, TILE * j:TILE * (j + 1)].reshape(TILE, TILE).astype(F32)
        zt[TILE * j:TILE * (j + 1), :] = jnp.transpose(turn)
    for g in range(4):
        ykv[g] = zt[KV * g:KV * (g + 1), :].astype(BF16)

    tiles_of = [y, lax.rem(y + 3, 4), lax.rem(y + 1, 4), lax.rem(y + 2, 4)]
    lanes_of = [pl.ds(pl.multiple_of(BLOCK + t * TILE, TILE), TILE) for t in tiles_of]
    ycopies = []
    for d in ORDER:
        yc = remote(ykv.at[lax.rem(y + d, 4)], kvbuf.at[x, 0:KV, lanes_of[0]], YK + d - 1, ypeer(d))
        yc.start()
        ycopies.append(yc)
    kvbuf[x, 0:KV, lanes_of[0]] = ykv[y]

    frames = (x, x - 1, x + 1)
    lives = (x >= 0, x > 0, x < 3)
    up, down = p < 7, p > 0

    def pass_on(side, rel, k):
        src = kvbuf.at[frames[rel], 0:KV, lanes_of[k]]
        shift = -BLOCK if side == 0 else BLOCK
        lanes = pl.ds(pl.multiple_of(BLOCK + shift + tiles_of[k] * TILE, TILE), TILE)
        return remote(src, kvbuf.at[frames[rel], 0:KV, lanes], PF + (side * 3 + rel) * 4 + k,
                      (seq + 1 - 2 * side, head))

    def pass_tile(rel, k):
        for side, gate_on in ((0, up), (1, down)):
            @pl.when(lives[rel] & gate_on)
            def _():
                pass_on(side, rel, k).start()

    xcopies = {}
    for k in range(4):
        if k:
            ycopies[k - 1].wait()
        for d in ORDER:
            ref = kvbuf.at[x, 0:KV, lanes_of[k]]
            xcopies[d, k] = remote(ref, ref, X0 + 4 * (d - 1) + k, xpeer(d))
            xcopies[d, k].start()
        pass_tile(0, k)

    for zc in zb:
        zc.wait()
    for j in range((GPAD - CUT) // TILE):
        turn = zrb[:, :, TILE * j:TILE * (j + 1)].reshape(TILE, TILE).astype(F32)
        zt[CUT + TILE * j:CUT + TILE * (j + 1), :] = jnp.transpose(turn)
    for g in range(4):
        row = 4 * KV + HD * g
        yq[g] = jnp.concatenate([zt[row:row + HD, :], jnp.zeros((8, TILE), F32)], axis=0).astype(BF16)
    qcopies = []
    for d in ORDER:
        qc = remote(yq.at[lax.rem(y + d, 4)], qbuf.at[y], YQ + d - 1, ypeer(d))
        qc.start()
        qcopies.append(qc)
    qbuf[y] = yq[y]

    def attend(frame, tiles, first):
        @pl.loop(0, 4, unroll=2)
        def _(a):
            lead = 4 if tiles == 9 else 0
            base = a + 4 - lead
            lanes = pl.ds(pl.multiple_of(base * TILE, TILE), tiles * TILE)
            q = qs[a]
            s = jnp.dot(q, kvbuf[frame, 0:TILE, lanes], preferred_element_type=F32)
            top = None
            pens = []
            for t in range(tiles):
                spot = 4 * p + a - lead + t
                inside = (spot >= 0) & (spot < 32)
                live = mask_ref[4 * lax.rem(seq, 2) + a, frame * 32 + jnp.clip(spot, 0, 31)]
                pen = jnp.where(inside, jnp.where(live > 0, 0.0, FAR), FAR).astype(F32)
                pens.append(pen)
                val = s[:, t * TILE:(t + 1) * TILE] - pen
                top = val if top is None else jnp.maximum(top, val)
            m = jnp.max(top, axis=1, keepdims=True)
            if not first:
                old = mrun[a][:, 0:1]
                m = jnp.maximum(m, old)
            mc = m * C_EXP
            weights = jnp.concatenate(
                [jnp.exp2(s[:, t * TILE:(t + 1) * TILE] * C_EXP - (mc + pens[t])).astype(BF16)
                 for t in range(tiles)], axis=1)
            got = lax.dot_general(weights, kvbuf[frame, :, lanes], (((1,), (1,)), ((), ())),
                                  preferred_element_type=F32)
            if first:
                acc[a, :, 0:KVR] = got
            else:
                acc[a, :, 0:KVR] = acc[a, :, 0:KVR] * jnp.exp2((old - m) * C_EXP) + got
            mrun[a] = jnp.broadcast_to(m, (TILE, TILE))

    for k in range(4):
        for rel, d in ((1, 1), (2, 3)):
            xcopies[d, k].wait_recv()
            pass_tile(rel, k)

    for qc in qcopies:
        qc.wait()
    for a in range(4):
        padded = jnp.concatenate([qbuf[a].astype(F32), jnp.zeros((48, TILE), F32)], axis=0)
        qs[a] = jnp.transpose(padded).astype(BF16)

    for w in wz:
        w.wait()
    group = wall.at[c, x]
    wx = {d: remote(group, group, WX + d - 1, xpeer(d)) for d in ORDER}
    for d in ORDER:
        wx[d].start()
    other = (seq + 1 - 2 * c, head)
    wc = [remote(group, group, WC, other)]
    wc[0].start()

    def passed(rel):
        for side, gate_on in ((0, down), (1, up)):
            @pl.when(lives[rel] & gate_on)
            def _():
                for k in range(4):
                    pass_on(side, rel, k).wait_recv()

    passed(0)

    attend(x, 9, True)

    for k in range(4):
        xcopies[2, k].wait_recv()
    attend(lax.rem(x + 2, 4), 1, False)

    passed(1)

    @pl.when(x > 0)
    def _():
        attend(x - 1, 9, False)

    @pl.when(x == 0)
    def _():
        attend(3, 1, False)

    passed(2)

    @pl.when(x < 3)
    def _():
        attend(x + 1, 9, False)

    @pl.when(x == 3)
    def _():
        attend(0, 1, False)

    def finished(g):
        rows = acc[:, pl.ds(pl.multiple_of(32 * g, 32), 32), :].reshape(TILE, 2 * TILE)
        low = jnp.transpose(rows[:, 0:TILE])
        high = jnp.transpose(rows[:, TILE:2 * TILE])
        total = high[KV - TILE:KV - TILE + 1]
        feats = jnp.concatenate([low[HD:TILE], high[0:KV - TILE]], axis=0) / total
        return jnp.concatenate([feats, jnp.zeros((8, TILE), F32)], axis=0).astype(BF16)

    bcopies = []
    for d in (2, 1, 3):
        dest = lax.rem(zh + d, 4)
        bsend[d] = finished(dest)
        bc = remote(bsend.at[d], brecv.at[zh], B0 + d - 1, zpeer(d))
        bc.start()
        bcopies.append(bc)
    brecv[zh] = finished(zh)

    for n, d in enumerate(ORDER):
        wx[d].wait()
        got_x = wall.at[c, lax.rem(x + 4 - d, 4)]
        wc.append(remote(got_x, got_x, WC + 1 + n, other))
        wc[-1].start()
    for n, d in enumerate((0,) + ORDER):
        wc[n].wait()
        frm = lax.rem(x + 4 - d, 4)
        for s in range(8):
            piece = wall[s % 2, frm, s // 2]
            wfull[COLS * s:COLS * (s + 1), :] = piece[0:COLS].astype(F32)
        wt[pl.ds(pl.multiple_of(288 * frm, 32), 288), :] = wfull[...].astype(BF16)

    for bc in bcopies:
        bc.wait()

    feats = jnp.concatenate(
        [brecv[...].reshape(320, TILE).astype(F32), jnp.zeros((64, TILE), F32)], axis=0)
    att = jnp.concatenate(
        [jnp.transpose(feats[TILE * j:TILE * (j + 1)]) for j in range(3)], axis=1).astype(BF16)
    rcopies = []
    for j in range(3):
        res = lax.dot_general(att, wt[384 * j:384 * (j + 1)], (((1,), (1,)), ((), ())),
                              preferred_element_type=F32)
        part[j] = res
        for g in range(4):
            psend[j, g] = res[32 * g:32 * (g + 1)].astype(BF16)
        for d in (2, 1, 3):
            rc = remote(psend.at[j, lax.rem(y + d, 4)], precv.at[j, d - 1], R0 + 3 * j + d - 1, ypeer(d))
            rc.start()
            rcopies.append(rc)

    for j in range(3):
        for rc in rcopies[3 * j:3 * j + 3]:
            rc.wait()
        cols = slice(384 * j, 384 * (j + 1))
        proj = part[j, pl.ds(pl.multiple_of(32 * y, 32), 32), :] + bias_ref[cols].reshape(1, -1)
        for d in range(3):
            proj = proj + precv[j, d].astype(F32)
        out_ref[:, cols] = (tok_ref[:, cols].astype(F32) + gate_row[0:1, cols] * proj).astype(BF16)

    for copy in xcopies.values():
        copy.wait_send()
    for rel in range(3):
        for side, gate_on in ((0, up), (1, down)):
            @pl.when(lives[rel] & gate_on)
            def _():
                for k in range(4):
                    pass_on(side, rel, k).wait_send()


def shards(tokens, qkv, out_weight, out_bias, gate_table, timesteps, tile_mask):
    d = tokens.shape[1]
    vm = pl.BlockSpec(memory_space=pltpu.VMEM)
    hbm = pl.BlockSpec(memory_space=pltpu.HBM)
    return pl.pallas_call(
        body,
        out_shape=jax.ShapeDtypeStruct(tokens.shape, BF16),
        in_specs=[hbm] * 7,
        out_specs=vm,
        scratch_shapes=[
            pltpu.VMEM(tokens.shape, BF16),
            pltpu.VMEM(qkv.shape, BF16),
            pltpu.VMEM(out_weight.shape[::-1], BF16),
            pltpu.VMEM((d,), F32),
            pltpu.SMEM(timesteps.shape, jnp.int32),
            pltpu.SMEM((8, tile_mask.shape[1]), jnp.int32),
            pltpu.VMEM((4, 32, CUT), BF16),
            pltpu.VMEM((4, 32, GPAD - CUT), BF16),
            pltpu.VMEM((4, 32, CUT), BF16),
            pltpu.VMEM((4, 32, GPAD - CUT), BF16),
            pltpu.VMEM((GPAD, TILE), F32),
            pltpu.VMEM((4, KV, TILE), BF16),
            pltpu.VMEM((4, 80, TILE), BF16),
            pltpu.VMEM((4, 80, TILE), BF16),
            pltpu.VMEM((4, TILE, TILE), BF16),
            pltpu.VMEM((4, KVR, 3 * BLOCK), BF16),
            pltpu.VMEM((4, TILE, 2 * TILE), F32),
            pltpu.VMEM((4, TILE, TILE), F32),
            pltpu.VMEM((4, 80, TILE), BF16),
            pltpu.VMEM((4, 80, TILE), BF16),
            pltpu.VMEM((48, d), F32),
            pltpu.VMEM((2, 4, 4, 48, 384), BF16),
            pltpu.VMEM((288, 384), F32),
            pltpu.VMEM((d, 384), BF16),
            pltpu.VMEM((3, TILE, 384), F32),
            pltpu.VMEM((3, 4, 32, 384), BF16),
            pltpu.VMEM((3, 3, 32, 384), BF16),
            pltpu.VMEM(gate_table.shape, BF16),
            pltpu.VMEM((16, d), F32),
            pltpu.SemaphoreType.DMA((NSEM,)),
            pltpu.SemaphoreType.DMA((NSEM,)),
            pltpu.SemaphoreType.DMA((7,)),
        ],
        compiler_params=pltpu.CompilerParams(
            collective_id=0, has_side_effects=True, vmem_limit_bytes=40 * 1024 * 1024),
    )(*[pltpu.with_memory_space_constraint(a, pltpu.HBM) for a in (
        tokens, qkv, out_weight.T, out_bias, gate_table, timesteps, tile_mask)])


def solution(mesh):
    return jax.shard_map(
        shards,
        mesh=mesh,
        in_specs=(
            P(("seq", "head"), None),
            P(("seq", "head"), None),
            P(None, "seq"),
            P(),
            P(),
            P(),
            P(),
        ),
        out_specs=P(("seq", "head"), None),
        check_vma=False,
    )
```

```python
import functools
import math

import jax
import jax.numpy as jnp
from jax import lax
from jax.experimental import pallas as pl
from jax.experimental.pallas import tpu as pltpu
from jax.sharding import PartitionSpec as P

F32 = jnp.float32
BF16 = jnp.bfloat16
MESH = pl.DeviceIdType.MESH

HD = 72
TILE = 128
BLOCK = 512
KV = 2 * HD
KVR = KV + 16
GROUP = 4 * 3 * HD
GPAD = 896
CUT = 640
COLS = 36
FAR = 1e30
C_EXP = HD ** (-0.5) * math.log2(math.e)

ZA, ZB, YK, YQ, X0, PF, WZ, WX, WC, B0, R0, NSEM = 0, 3, 6, 9, 12, 24, 48, 51, 54, 58, 61, 64
ORDER = (1, 3, 2)


def body(tok_hbm, qkv_hbm, w_hbm, bias_hbm, gate_hbm, ts_hbm, mask_hbm, out_ref,
         tok_ref, qkv_ref, w_ref, bias_ref, ts_ref, mask_ref, zsa, zsb, zra, zrb, zt, ykv, yq, qbuf, qs,
         kvbuf, acc, mrun, bsend, brecv, wf, wall, wfull, wt, part, psend, precv, gate_v, gate_row,
         send_sem, recv_sem, in_sem):
    seq = lax.axis_index("seq")
    head = lax.axis_index("head")
    x = seq // 8
    p = lax.rem(seq, 8)
    zl = p // 2
    c = lax.rem(p, 2)
    y = head // 4
    zh = lax.rem(head, 4)
    z = zh * 4 + zl

    def at_z(new_z, core):
        nz = lax.rem(new_z + 16, 16)
        return (x * 8 + lax.rem(nz, 4) * 2 + core, y * 4 + nz // 4)

    def zpeer(d):
        return (seq, y * 4 + lax.rem(zh + d, 4))

    def ypeer(d):
        return (seq, lax.rem(y + d, 4) * 4 + zh)

    def xpeer(d):
        return (lax.rem(x + d, 4) * 8 + p, head)

    def remote(src, dst, k, dev):
        return pltpu.make_async_remote_copy(
            src_ref=src, dst_ref=dst, send_sem=send_sem.at[k], recv_sem=recv_sem.at[k],
            device_id=dev, device_id_type=MESH)

    mask_row = pl.multiple_of((seq // 2) * 8, 8)
    loads = [pltpu.make_async_copy(src, dst, in_sem.at[k]) for k, (src, dst) in enumerate((
        (qkv_hbm, qkv_ref), (w_hbm, w_ref), (mask_hbm.at[pl.ds(mask_row, 8)], mask_ref), (ts_hbm, ts_ref),
        (gate_hbm, gate_v), (tok_hbm, tok_ref), (bias_hbm, bias_ref)))]
    for load in loads:
        load.start()

    barrier = pltpu.get_barrier_semaphore()
    far_z = jnp.where(c == 0, z + 2, z + 14)
    from_z = jnp.where(c == 0, z + 14, z + 2)
    peers = [f(d) for f in (zpeer, ypeer, xpeer) for d in (1, 2, 3)]
    peers += [at_z(z + 1, c), at_z(z + 15, c), at_z(far_z, c), at_z(from_z, c)]
    for dev in peers:
        pl.semaphore_signal(barrier, inc=1, device_id=dev, device_id_type=MESH)

    @pl.when(p > 0)
    def _():
        pl.semaphore_signal(barrier, inc=1, device_id=(seq - 1, head), device_id_type=MESH)

    @pl.when(p < 7)
    def _():
        pl.semaphore_signal(barrier, inc=1, device_id=(seq + 1, head), device_id_type=MESH)

    loads[0].wait()
    for g in range(4):
        first = (GROUP * g) // TILE
        off = GROUP * g - first * TILE
        tiles = -(-(off + GROUP) // TILE)
        piece = qkv_ref[:, first * TILE:(first + tiles) * TILE].astype(F32)
        starts = [off + 3 * HD * i for i in range(4)]
        cols = jnp.concatenate(
            [piece[:, a + HD:a + 3 * HD] for a in starts] + [piece[:, a:a + HD] for a in starts]
            + [jnp.zeros((piece.shape[0], GPAD - GROUP), F32)], axis=1)
        zsa[g] = cols[:, :CUT].astype(BF16)
        zsb[g] = cols[:, CUT:].astype(BF16)

    count = 13 + jnp.where(p > 0, 1, 0) + jnp.where(p < 7, 1, 0)
    pl.semaphore_wait(barrier, count)

    def start_z(src, dst, base):
        copies = []
        for d in (2, 1, 3):
            zc = remote(src.at[lax.rem(zh + d, 4)], dst.at[zh], base + d - 1, zpeer(d))
            zc.start()
            copies.append(zc)
        dst[zh] = src[zh]
        return copies

    za = start_z(zsa, zra, ZA)

    loads[1].wait()
    wf[COLS:48, :] = jnp.zeros((48 - COLS, wf.shape[1]), F32)
    wf[0:COLS, :] = w_ref[...].astype(F32)
    wide = wf[...]
    lane = lax.broadcasted_iota(jnp.int32, (48, 384), 1)
    shard = jnp.zeros((48, 384), F32)
    for g in range(4):
        turned = pltpu.roll(wide, lax.rem(wf.shape[1] + 80 * g - (g * 4 + y) * HD, wf.shape[1]), 1)[:, 0:384]
        shard = jnp.where((lane >= 80 * g) & (lane < 80 * g + HD), turned, shard)
    wall[c, x, zl] = shard.astype(BF16)
    own_shard = wall.at[c, x, zl]
    wz = [remote(own_shard, own_shard, WZ, at_z(z + 1, c)),
          remote(own_shard, own_shard, WZ + 1, at_z(z + 15, c)),
          remote(own_shard, own_shard, WZ + 2, at_z(far_z, c))]

    for w in wz:
        w.start()
    for f in range(4):
        kvbuf[f, KV:KVR, :] = jnp.ones((KVR - KV, 3 * BLOCK), BF16)

    @pl.when(p == 0)
    def _():
        for f in range(4):
            kvbuf[f, 0:KV, 0:BLOCK] = jnp.zeros((KV, BLOCK), BF16)

    @pl.when(p == 7)
    def _():
        for f in range(4):
            kvbuf[f, 0:KV, 2 * BLOCK:3 * BLOCK] = jnp.zeros((KV, BLOCK), BF16)

    for load in loads[2:]:
        load.wait()
    step = ts_ref[x]
    one_hot = (lax.broadcasted_iota(jnp.int32, (16, 1000), 1) == step).astype(F32).astype(BF16)
    gate_row[...] = jnp.dot(one_hot, gate_v[...], preferred_element_type=F32)

    for zc in za:
        zc.wait_send()
    zb = start_z(zsb, zrb, ZB)
    for zc in za:
        zc.wait_recv()

    for j in range(CUT // TILE):
        turn = zra[:, :, TILE * j:TILE * (j + 1)].reshape(TILE, TILE).astype(F32)
        zt[TILE * j:TILE * (j + 1), :] = jnp.transpose(turn)
    for g in range(4):
        ykv[g] = zt[KV * g:KV * (g + 1), :].astype(BF16)

    tiles_of = [y, lax.rem(y + 3, 4), lax.rem(y + 1, 4), lax.rem(y + 2, 4)]
    lanes_of = [pl.ds(pl.multiple_of(BLOCK + t * TILE, TILE), TILE) for t in tiles_of]
    ycopies = []
    for d in ORDER:
        yc = remote(ykv.at[lax.rem(y + d, 4)], kvbuf.at[x, 0:KV, lanes_of[0]], YK + d - 1, ypeer(d))
        yc.start()
        ycopies.append(yc)
    kvbuf[x, 0:KV, lanes_of[0]] = ykv[y]

    frames = (x, x - 1, x + 1)
    lives = (x >= 0, x > 0, x < 3)
    up, down = p < 7, p > 0

    def pass_on(side, rel, k):
        src = kvbuf.at[frames[rel], 0:KV, lanes_of[k]]
        shift = -BLOCK if side == 0 else BLOCK
        lanes = pl.ds(pl.multiple_of(BLOCK + shift + tiles_of[k] * TILE, TILE), TILE)
        return remote(src, kvbuf.at[frames[rel], 0:KV, lanes], PF + (side * 3 + rel) * 4 + k,
                      (seq + 1 - 2 * side, head))

    def pass_tile(rel, k):
        for side, gate_on in ((0, up), (1, down)):
            @pl.when(lives[rel] & gate_on)
            def _():
                pass_on(side, rel, k).start()

    xcopies = {}
    for k in range(4):
        if k:
            ycopies[k - 1].wait()
        for d in ORDER:
            ref = kvbuf.at[x, 0:KV, lanes_of[k]]
            xcopies[d, k] = remote(ref, ref, X0 + 4 * (d - 1) + k, xpeer(d))
            xcopies[d, k].start()
        pass_tile(0, k)

    for zc in zb:
        zc.wait()
    for j in range((GPAD - CUT) // TILE):
        turn = zrb[:, :, TILE * j:TILE * (j + 1)].reshape(TILE, TILE).astype(F32)
        zt[CUT + TILE * j:CUT + TILE * (j + 1), :] = jnp.transpose(turn)
    for g in range(4):
        row = 4 * KV + HD * g
        yq[g] = jnp.concatenate([zt[row:row + HD, :], jnp.zeros((8, TILE), F32)], axis=0).astype(BF16)
    qcopies = []
    for d in ORDER:
        qc = remote(yq.at[lax.rem(y + d, 4)], qbuf.at[y], YQ + d - 1, ypeer(d))
        qc.start()
        qcopies.append(qc)
    qbuf[y] = yq[y]

    def attend(frame, tiles, first):
        @pl.loop(0, 4, unroll=2)
        def _(a):
            lead = 4 if tiles == 9 else 0
            base = a + 4 - lead
            lanes = pl.ds(pl.multiple_of(base * TILE, TILE), tiles * TILE)
            q = qs[a]
            s = jnp.dot(q, kvbuf[frame, 0:TILE, lanes], preferred_element_type=F32)
            top = None
            pens = []
            for t in range(tiles):
                spot = 4 * p + a - lead + t
                inside = (spot >= 0) & (spot < 32)
                live = mask_ref[4 * lax.rem(seq, 2) + a, frame * 32 + jnp.clip(spot, 0, 31)]
                pen = jnp.where(inside, jnp.where(live > 0, 0.0, FAR), FAR).astype(F32)
                pens.append(pen)
                val = s[:, t * TILE:(t + 1) * TILE] - pen
                top = val if top is None else jnp.maximum(top, val)
            m = jnp.max(top, axis=1, keepdims=True)
            if not first:
                old = mrun[a][:, 0:1]
                m = jnp.maximum(m, old)
            mc = m * C_EXP
            weights = jnp.concatenate(
                [jnp.exp2(s[:, t * TILE:(t + 1) * TILE] * C_EXP - (mc + pens[t])).astype(BF16)
                 for t in range(tiles)], axis=1)
            got = lax.dot_general(weights, kvbuf[frame, :, lanes], (((1,), (1,)), ((), ())),
                                  preferred_element_type=F32)
            if first:
                acc[a, :, 0:KVR] = got
            else:
                acc[a, :, 0:KVR] = acc[a, :, 0:KVR] * jnp.exp2((old - m) * C_EXP) + got
            mrun[a] = jnp.broadcast_to(m, (TILE, TILE))

    for k in range(4):
        for rel, d in ((1, 1), (2, 3)):
            xcopies[d, k].wait_recv()
            pass_tile(rel, k)

    for qc in qcopies:
        qc.wait()
    for a in range(4):
        padded = jnp.concatenate([qbuf[a].astype(F32), jnp.zeros((48, TILE), F32)], axis=0)
        qs[a] = jnp.transpose(padded).astype(BF16)

    for w in wz:
        w.wait()
    group = wall.at[c, x]
    wx = {d: remote(group, group, WX + d - 1, xpeer(d)) for d in ORDER}
    for d in ORDER:
        wx[d].start()
    other = (seq + 1 - 2 * c, head)
    wc = [remote(group, group, WC, other)]
    wc[0].start()

    def passed(rel):
        for side, gate_on in ((0, down), (1, up)):
            @pl.when(lives[rel] & gate_on)
            def _():
                for k in range(4):
                    pass_on(side, rel, k).wait_recv()

    passed(0)

    attend(x, 9, True)

    for k in range(4):
        xcopies[2, k].wait_recv()
    attend(lax.rem(x + 2, 4), 1, False)

    passed(1)

    @pl.when(x > 0)
    def _():
        attend(x - 1, 9, False)

    @pl.when(x == 0)
    def _():
        attend(3, 1, False)

    passed(2)

    @pl.when(x < 3)
    def _():
        attend(x + 1, 9, False)

    @pl.when(x == 3)
    def _():
        attend(0, 1, False)

    def finished(g):
        rows = acc[:, pl.ds(pl.multiple_of(32 * g, 32), 32), :].reshape(TILE, 2 * TILE)
        low = jnp.transpose(rows[:, 0:TILE])
        high = jnp.transpose(rows[:, TILE:2 * TILE])
        total = high[KV - TILE:KV - TILE + 1]
        feats = jnp.concatenate([low[HD:TILE], high[0:KV - TILE]], axis=0) / total
        return jnp.concatenate([feats, jnp.zeros((8, TILE), F32)], axis=0).astype(BF16)

    bcopies = []
    for d in (2, 1, 3):
        dest = lax.rem(zh + d, 4)
        bsend[d] = finished(dest)
        bc = remote(bsend.at[d], brecv.at[zh], B0 + d - 1, zpeer(d))
        bc.start()
        bcopies.append(bc)
    brecv[zh] = finished(zh)

    for n, d in enumerate(ORDER):
        wx[d].wait()
        got_x = wall.at[c, lax.rem(x + 4 - d, 4)]
        wc.append(remote(got_x, got_x, WC + 1 + n, other))
        wc[-1].start()
    for n, d in enumerate((0,) + ORDER):
        wc[n].wait()
        frm = lax.rem(x + 4 - d, 4)
        for s in range(8):
            piece = wall[s % 2, frm, s // 2]
            wfull[COLS * s:COLS * (s + 1), :] = piece[0:COLS].astype(F32)
        wt[pl.ds(pl.multiple_of(288 * frm, 32), 288), :] = wfull[...].astype(BF16)

    for bc in bcopies:
        bc.wait()

    feats = jnp.concatenate(
        [brecv[...].reshape(320, TILE).astype(F32), jnp.zeros((64, TILE), F32)], axis=0)
    att = jnp.concatenate(
        [jnp.transpose(feats[TILE * j:TILE * (j + 1)]) for j in range(3)], axis=1).astype(BF16)
    rcopies = []
    for j in range(1):
        res = lax.dot_general(att, wt[1152 * j:1152 * (j + 1)], (((1,), (1,)), ((), ())),
                              preferred_element_type=F32)
        part[j] = res
        for g in range(4):
            psend[j, g] = res[32 * g:32 * (g + 1)].astype(BF16)
        for d in (2, 1, 3):
            rc = remote(psend.at[j, lax.rem(y + d, 4)], precv.at[j, d - 1], R0 + 3 * j + d - 1, ypeer(d))
            rc.start()
            rcopies.append(rc)

    for j in range(1):
        for rc in rcopies[3 * j:3 * j + 3]:
            rc.wait()
        cols = slice(1152 * j, 1152 * (j + 1))
        proj = part[j, pl.ds(pl.multiple_of(32 * y, 32), 32), :] + bias_ref[cols].reshape(1, -1)
        for d in range(3):
            proj = proj + precv[j, d].astype(F32)
        out_ref[:, cols] = (tok_ref[:, cols].astype(F32) + gate_row[0:1, cols] * proj).astype(BF16)

    for copy in xcopies.values():
        copy.wait_send()
    for rel in range(3):
        for side, gate_on in ((0, up), (1, down)):
            @pl.when(lives[rel] & gate_on)
            def _():
                for k in range(4):
                    pass_on(side, rel, k).wait_send()


def shards(tokens, qkv, out_weight, out_bias, gate_table, timesteps, tile_mask):
    d = tokens.shape[1]
    vm = pl.BlockSpec(memory_space=pltpu.VMEM)
    hbm = pl.BlockSpec(memory_space=pltpu.HBM)
    return pl.pallas_call(
        body,
        out_shape=jax.ShapeDtypeStruct(tokens.shape, BF16),
        in_specs=[hbm] * 7,
        out_specs=vm,
        scratch_shapes=[
            pltpu.VMEM(tokens.shape, BF16),
            pltpu.VMEM(qkv.shape, BF16),
            pltpu.VMEM(out_weight.shape[::-1], BF16),
            pltpu.VMEM((d,), F32),
            pltpu.SMEM(timesteps.shape, jnp.int32),
            pltpu.SMEM((8, tile_mask.shape[1]), jnp.int32),
            pltpu.VMEM((4, 32, CUT), BF16),
            pltpu.VMEM((4, 32, GPAD - CUT), BF16),
            pltpu.VMEM((4, 32, CUT), BF16),
            pltpu.VMEM((4, 32, GPAD - CUT), BF16),
            pltpu.VMEM((GPAD, TILE), F32),
            pltpu.VMEM((4, KV, TILE), BF16),
            pltpu.VMEM((4, 80, TILE), BF16),
            pltpu.VMEM((4, 80, TILE), BF16),
            pltpu.VMEM((4, TILE, TILE), BF16),
            pltpu.VMEM((4, KVR, 3 * BLOCK), BF16),
            pltpu.VMEM((4, TILE, 2 * TILE), F32),
            pltpu.VMEM((4, TILE, TILE), F32),
            pltpu.VMEM((4, 80, TILE), BF16),
            pltpu.VMEM((4, 80, TILE), BF16),
            pltpu.VMEM((48, d), F32),
            pltpu.VMEM((2, 4, 4, 48, 384), BF16),
            pltpu.VMEM((288, 384), F32),
            pltpu.VMEM((d, 384), BF16),
            pltpu.VMEM((1, TILE, 1152), F32),
            pltpu.VMEM((1, 4, 32, 1152), BF16),
            pltpu.VMEM((1, 3, 32, 1152), BF16),
            pltpu.VMEM(gate_table.shape, BF16),
            pltpu.VMEM((16, d), F32),
            pltpu.SemaphoreType.DMA((NSEM,)),
            pltpu.SemaphoreType.DMA((NSEM,)),
            pltpu.SemaphoreType.DMA((7,)),
        ],
        compiler_params=pltpu.CompilerParams(
            collective_id=0, has_side_effects=True, vmem_limit_bytes=40 * 1024 * 1024),
    )(*[pltpu.with_memory_space_constraint(a, pltpu.HBM) for a in (
        tokens, qkv, out_weight.T, out_bias, gate_table, timesteps, tile_mask)])


def solution(mesh):
    return jax.shard_map(
        shards,
        mesh=mesh,
        in_specs=(
            P(("seq", "head"), None),
            P(("seq", "head"), None),
            P(None, "seq"),
            P(),
            P(),
            P(),
            P(),
        ),
        out_specs=P(("seq", "head"), None),
        check_vma=False,
    )
```
